256 devices in a mesh: dp: 4 (over x), expert: 64 (over z, y, core).
Axes of the slice: x: 4, y: 4, z: 8, core: 2. Of those that a mesh axis runs over, the one named last changes fastest.
Arguments:
- tokens: bfloat16 [32768, 4096], P(('dp', 'expert')), may hold values from -6 to 6
- cotangent: bfloat16 [32768, 4096], P(('dp', 'expert')), may hold values from -1.5 to 1.5
- expert_ids: int32 [32768, 2], P(('dp', 'expert')), may hold values from 0 to 63, all different within a row; in each aligned block of 128 rows (0 to 127, 128 to 255, ...) at most 6 rows name the same one
- gates: bfloat16 [32768, 2], P(('dp', 'expert')), may hold values from 0.099609375 to 1
- widths: int32 [64], replicated, may hold values from 64 to 512, as said below
- placement: int32 [64], replicated, may hold values from 0 to 63, each once
- w_gate: bfloat16 [64, 4096, 512], P('expert', 'dp'), may hold values from -0.09375 to 0.09375
- w_up: bfloat16 [64, 4096, 512], P('expert', 'dp'), may hold values from -0.09375 to 0.09375
- w_down: bfloat16 [64, 512, 4096], P('expert', None, 'dp'), may hold values from -0.375 to 0.375
Outputs:
- grad_tokens: bfloat16 [32768, 4096], P(('dp', 'expert'))
- grad_gate: bfloat16 [64, 4096, 512], P('expert', 'dp')
- grad_up: bfloat16 [64, 4096, 512], P('expert', 'dp')
- grad_down: bfloat16 [64, 512, 4096], P('expert', None, 'dp')
The draws below stay inside these ranges and needn't reach their ends.
Inputs may be any that keep to these rules, and one draw needn't show every extreme that they name: `expert_ids`: among the 128 tokens of one device (aligned blocks of rows), no expert is named by more than 6 choices, and in some block one expert is named by exactly 6; a token's two experts differ. `widths`: multiples of 64; some expert has 512. `placement`: each slot holds one expert.
All inputs are finite; a program needn't handle non-finite values.
Results may differ from the reference program's by a relative error of at most 0.013.
Values may be sent and summed in bfloat16 or wider, within the bound.
No kernel may reach another device: no remote copies, remote signals or barrier semaphores. Data moves between devices by JAX's collectives and lax.ppermute only.
A program may use at most 128 MiB of HBM per device.

```python
import math
import jax
import jax.numpy as jnp
import numpy as np
from jax import lax

D = 4096
HMAX = 512
TOK_DEV = 128
EXPERTS = 64
CAP = 6
TOKENS = 32768
N_DP = 4
N_EXPERT = 64


def draw_widths(key, part):
    key = jax.random.fold_in(key, 11)
    first_key, second_key = jax.random.split(key)
    levels = jax.random.randint(first_key, (EXPERTS,), 1, HMAX // 64 + 1)
    chosen = jax.random.randint(second_key, (), 0, EXPERTS)
    levels = jnp.where(jnp.arange(EXPERTS) == chosen, HMAX // 64, levels)
    return (levels * 64).astype(jnp.int32)


def steps_of(own_key, shape, pieces, smallest, largest):
    def one(position, parts):
        draws = jax.random.uniform(jax.random.fold_in(jax.random.fold_in(own_key, 6), position), (parts,), jnp.float32, smallest / len(pieces), largest / len(pieces))
        return jnp.repeat(jnp.exp(draws), shape[position] // parts).reshape((-1,) + (1,) * (len(shape) - position - 1))

    gain = one(*pieces[0])
    for cut in pieces[1:]:
        gain = gain * one(*cut)
    return gain


def assign_block(rng, own, number, rows, count, top, reach, skew):
    sequence = jax.random.permutation(rng, count)
    heavy_load, usual = load_shares(count, rows * top, reach, skew, True), load_shares(count, rows * top, reach, skew, False)
    places = jnp.arange(count)

    def named(lengths, rotation):
        used = int((lengths > 0).sum())
        fixed = max(1, used // 4)
        shifted = fixed + (places - fixed + rotation * (used - fixed)) % max(1, count - fixed)
        return jnp.zeros((count,), jnp.int32).at[sequence[jnp.where(places < fixed, places, shifted)]].set(jnp.asarray(lengths, jnp.int32))

    lengths = jnp.where(number % 4 == 0, named(heavy_load, number // 4), named(usual, number - number // 4 - 1))
    mixed = jax.random.permutation(jax.random.fold_in(own, 3), count)
    source_of, taker = mixed[0:count // 2 * 2:2], mixed[1:count // 2 * 2:2]
    room = jnp.minimum(lengths[source_of] - 1, reach - lengths[taker]) // 2
    room = jnp.where((source_of == sequence[0]) | (taker == sequence[0]) | (lengths[taker] == 0), 0, jnp.maximum(room, 0))
    shifted = jax.random.randint(jax.random.fold_in(own, 4), (count // 2,), 0, 1 << 20) % (room + 1)
    lengths = lengths.at[source_of].add(-shifted).at[taker].add(shifted)
    labels = jnp.searchsorted(jnp.cumsum(lengths), jnp.arange(rows * top), side="right").astype(jnp.int32)
    table = labels.reshape(top, rows).T
    table = table[jax.random.permutation(jax.random.fold_in(own, 1), rows)]
    rotation = jax.random.randint(jax.random.fold_in(own, 2), (rows, 1), 0, top)
    return jnp.take_along_axis(table, (jnp.arange(top)[None, :] + rotation) % top, axis=1)


def load_shares(amount, total, reach, slope, full):
    portions = [(1 << 20) // math.isqrt(grade ** slope) + 1 for grade in range(1, amount + 1)]
    largest = reach if full else min(reach, max(-(-total // amount), total * portions[0] // sum(portions)))
    least = 1 if total - largest >= amount - 1 else 0
    holding, spare = [largest] + [least] * (amount - 1), total - largest - least * (amount - 1)
    while spare > 0:
        free = [i for i in range(1, amount) if holding[i] < largest] or [i for i in range(1, amount) if holding[i] < reach]
        whole, budget = sum([portions[i] for i in free]), spare
        for i in free:
            addition = min(reach - holding[i], max(1, budget * portions[i] // whole), spare)
            holding[i] = holding[i] + addition
            spare = spare - addition
    return np.array(holding)


def bell_draw(own_key, shape, deviation, reach, shards=(), held_as=jnp.bfloat16):
    level = steps_of(own_key, shape, shards, -0.22, 0.18) if shards else 1.0
    entries = jax.random.normal(own_key, shape, jnp.float32) * deviation * level
    return jnp.minimum(jnp.maximum(entries, -reach), reach).astype(held_as)


def setup_inputs(seed: int = 0) -> dict:
    arg_keys = jax.random.split(jax.random.key(seed), 10)
    tokens = bell_draw(arg_keys[0], (TOKENS, D), 1.0, 6.0, ((0, 256),))
    cotangent = bell_draw(arg_keys[1], (TOKENS, D), 0.25, 1.5, ((0, 256),))
    expert_ids_keys = jax.random.split(jax.random.fold_in(arg_keys[2], 1), TOKENS // TOK_DEV)
    expert_ids_turns = jax.random.permutation(jax.random.fold_in(arg_keys[2], 3), TOKENS // TOK_DEV)
    expert_ids = jax.vmap(lambda own, number: assign_block(jax.random.fold_in(arg_keys[2], 2), own, number, TOK_DEV, EXPERTS, 2, CAP, 2))(expert_ids_keys, expert_ids_turns).reshape((TOKENS, 2))
    gates = jnp.clip(0.099609375 + 0.9003906 * jax.random.uniform(arg_keys[3], (TOKENS, 2), jnp.float32) ** steps_of(arg_keys[3], (TOKENS, 2), ((0, 256),), -0.2, 0.2), 0.099609375, 1.0).astype(jnp.bfloat16)
    widths = draw_widths(jax.random.fold_in(arg_keys[9], 71), 0)
    placement = jax.random.permutation(arg_keys[5], EXPERTS).astype(jnp.int32)
    w_gate = bell_draw(arg_keys[6], (EXPERTS, D, HMAX), D ** -0.5, 0.09375, ((0, 64), (1, 4)))
    w_up = bell_draw(arg_keys[7], (EXPERTS, D, HMAX), D ** -0.5, 0.09375, ((0, 64), (1, 4)))
    w_down = bell_draw(arg_keys[8], (EXPERTS, HMAX, D), (HMAX // 2) ** -0.5, 0.375, ((0, 64), (2, 4)))
    return dict(tokens=tokens, cotangent=cotangent, expert_ids=expert_ids, gates=gates, widths=widths, placement=placement, w_gate=w_gate, w_up=w_up, w_down=w_down)


def expert_rows(rows_x, rows_g, gate_w, up_w, down_w, live_mask):
    pre_gate = jnp.dot(rows_x, gate_w, preferred_element_type=jnp.float32)
    pre_up = jnp.dot(rows_x, up_w, preferred_element_type=jnp.float32)
    sigmoid_gate = jax.nn.sigmoid(pre_gate)
    activated = pre_gate * sigmoid_gate
    hidden = jnp.where(live_mask, activated * pre_up, 0.0).astype(jnp.bfloat16)
    hidden_grad = jnp.where(live_mask, jnp.dot(rows_g, down_w.T, preferred_element_type=jnp.float32), 0.0)
    d_gate = (hidden_grad * pre_up * sigmoid_gate * (1.0 + pre_gate * (1.0 - sigmoid_gate))).astype(jnp.bfloat16)
    d_up = (hidden_grad * activated).astype(jnp.bfloat16)
    d_rows = (jnp.dot(d_gate, gate_w.T, preferred_element_type=jnp.float32)
              + jnp.dot(d_up, up_w.T, preferred_element_type=jnp.float32)).astype(jnp.bfloat16)
    return hidden, d_gate, d_up, d_rows


def rounded(value):
    return lax.optimization_barrier(value.astype(jnp.bfloat16)).astype(jnp.float32)


def reference(tokens, cotangent, expert_ids, gates, widths, placement, w_gate, w_up, w_down):
    group = N_EXPERT * TOK_DEV
    capacity = N_EXPERT * CAP
    expert_range = jnp.arange(EXPERTS, dtype=jnp.int32)
    unit_range = jnp.arange(HMAX, dtype=jnp.int32)

    def per_slot(grad_total, inputs):
        gate_w, up_w, down_w, slot = inputs
        owner = jnp.sum(jnp.where(placement == slot, expert_range, 0))
        width = jnp.sum(jnp.where(expert_range == owner, widths, 0))
        live_mask = (unit_range < width)[None, :]
        sums_gate = jnp.zeros((D, HMAX), jnp.float32)
        sums_up = jnp.zeros((D, HMAX), jnp.float32)
        sums_down = jnp.zeros((D, HMAX), jnp.float32)
        for member in range(N_DP):
            ids_part = expert_ids[member * group:(member + 1) * group]
            gate_part = gates[member * group:(member + 1) * group].reshape(-1)
            matched = (ids_part == owner).reshape(-1)
            ranks = jnp.cumsum(matched.astype(jnp.int32)) - 1
            where_to = jnp.where(matched, ranks, capacity).astype(jnp.int32)
            picked = jnp.zeros((capacity,), jnp.int32).at[where_to].set(
                jnp.arange(2 * group, dtype=jnp.int32), mode="drop")
            live_rows = (jnp.arange(capacity, dtype=jnp.int32) < jnp.sum(matched.astype(jnp.int32)))[:, None]
            token_index = (picked // 2 + member * group).astype(jnp.int32)
            rows_x = jnp.where(live_rows, tokens[token_index].astype(jnp.float32), 0.0).astype(jnp.bfloat16)
            scale_rows = gate_part[picked].astype(jnp.float32)[:, None]
            rows_g = jnp.where(live_rows, scale_rows * cotangent[token_index].astype(jnp.float32), 0.0).astype(jnp.bfloat16)
            hidden, d_gate, d_up, d_rows = expert_rows(rows_x, rows_g, gate_w, up_w, down_w, live_mask)
            sums_gate = sums_gate + rounded(jnp.dot(rows_x.T, d_gate, preferred_element_type=jnp.float32))
            sums_up = sums_up + rounded(jnp.dot(rows_x.T, d_up, preferred_element_type=jnp.float32))
            sums_down = sums_down + rounded(jnp.dot(rows_g.T, hidden, preferred_element_type=jnp.float32))
            grad_total = grad_total.at[token_index].add(jnp.where(live_rows, d_rows.astype(jnp.float32), 0.0))
        return grad_total, (sums_gate.astype(jnp.bfloat16), sums_up.astype(jnp.bfloat16), sums_down.T.astype(jnp.bfloat16))

    start_total = jnp.zeros((TOKENS, D), jnp.float32)
    grad_total, (grad_gate, grad_up, grad_down) = lax.scan(per_slot, start_total, (w_gate, w_up, w_down, expert_range))
    return grad_total.astype(jnp.bfloat16), grad_gate, grad_up, grad_down
```

```python
import functools

import jax
import jax.numpy as jnp
from jax import lax
from jax.experimental import pallas as pl
from jax.experimental.pallas import tpu as pltpu
from jax.sharding import PartitionSpec as P

BF = jnp.bfloat16
F32 = jnp.float32
SHARDS = 4
SLOTS = 6
PIECES = 3
CORES = 64
TOK = 128
WIDE = 1024
HID = 512
ROWS = CORES * SLOTS
PACKED = CORES * 8
VMEM = pl.BlockSpec(memory_space=pltpu.VMEM)
SMEM = pl.BlockSpec(memory_space=pltpu.SMEM)
ANY = pl.BlockSpec(memory_space=pl.ANY)
LIMIT = 56 * 1024 * 1024


def iota(shape, dim):
    return lax.broadcasted_iota(jnp.int32, shape, dim)


def cost(flops, nbytes):
    return pl.CostEstimate(flops=flops, bytes_accessed=nbytes, transcendentals=0)


def spread(rows):
    chunk = (iota((PACKED, TOK), 0) % 8) // 2
    return jnp.concatenate(
        [jnp.where(chunk == c, rows, 0.0).astype(BF) for c in range(SHARDS)], axis=1
    )


def stacked(ref):
    return jnp.concatenate([ref[:, c * WIDE : (c + 1) * WIDE] for c in range(SHARDS)], axis=0)


def route_kernel(ids, gates, place, tok, send, move, scale, hot_s, count_s, gate_s, tok_s):
    piece = pl.program_id(0)

    @pl.when(piece == 0)
    def _():
        expert = iota((CORES, TOK), 0)
        slot_of = (iota((CORES, CORES), 0) == place[0:1, :]).astype(BF)
        hot = [
            jnp.dot(slot_of, (ids[k : k + 1, :] == expert).astype(BF), preferred_element_type=F32)
            for k in range(2)
        ]
        both = hot[0] + hot[1]
        before = (iota((TOK, TOK), 0) < iota((TOK, TOK), 1)).astype(BF)
        count = jnp.dot(both.astype(BF), before, preferred_element_type=F32)
        gate = hot[0] * gates[0:1, :] + hot[1] * gates[1:2, :]
        for src, dst in ((both, hot_s), (count, count_s), (gate, gate_s)):
            dst[...] = jnp.broadcast_to(src[:, None, :], (CORES, 8, TOK)).reshape(PACKED, TOK)
        tok_s[...] = stacked(tok)

    slot = 2 * piece + iota((PACKED, TOK), 0) % 2
    here = count_s[...] == slot.astype(F32)
    rows = jnp.where(here, hot_s[...], 0.0)
    move[...] = rows.astype(BF)
    scale[...] = jnp.where(here, gate_s[...], 0.0).astype(BF)
    send[...] = jnp.dot(spread(rows), tok_s[...], preferred_element_type=F32).astype(BF)


def send_kernel(scale, cot, send, cot_s):
    @pl.when(pl.program_id(0) == 0)
    def _():
        cot_s[...] = stacked(cot)

    rows = scale[...].astype(F32)
    send[...] = jnp.dot(spread(rows), cot_s[...], preferred_element_type=F32).astype(BF)


def combine_kernel(move, back, out, acc):
    piece = pl.program_id(0)
    part = lax.dot_general(
        spread(move[...].astype(F32)),
        back[...],
        (((0,), (0,)), ((), ())),
        preferred_element_type=F32,
    )

    @pl.when(piece == 0)
    def _():
        acc[...] = part

    @pl.when(piece > 0)
    def _():
        acc[...] += part

    @pl.when(piece == PIECES - 1)
    def _():
        for c in range(SHARDS):
            out[:, c * WIDE : (c + 1) * WIDE] = acc[c * TOK : (c + 1) * TOK, :].astype(BF)


def packing(member, turned):
    shape = (256, 256)
    outer, inner = iota(shape, 1 if turned else 0), iota(shape, 0 if turned else 1)
    within = outer % 64
    chunk = (member + outer // 64) % SHARDS
    return (inner == (within // 2) * 8 + chunk * 2 + within % 2).astype(BF)


def unpack(packed, order, rows):
    for piece in range(PIECES):
        for half in range(2):
            block = jnp.dot(
                order,
                packed[half * 256 : half * 256 + 256, piece * WIDE : (piece + 1) * WIDE],
                preferred_element_type=F32,
            ).astype(BF)
            start = (piece * 2 + half) * 64
            for k in range(SHARDS):
                rows[start : start + 64, k * WIDE : (k + 1) * WIDE] = block[k * 64 : k * 64 + 64, :]


def copies_of(parts, dest, sems, base):
    own, right, opp_a, opp_b, left = parts
    half = opp_a.shape[0]
    pairs = (
        (own, dest.at[0]),
        (right, dest.at[1]),
        (left, dest.at[3]),
        (opp_a, dest.at[2, pl.ds(0, half)]),
        (opp_b, dest.at[2, pl.ds(half, half)]),
    )
    return [pltpu.make_async_copy(s, d, sems.at[base + n]) for n, (s, d) in enumerate(pairs)]


def forward_kernel(info, recv, *refs):
    gate_parts, up_parts = refs[0:5], refs[5:10]
    rows, hidden, slope_gate, slope_up = refs[10:14]
    recv_v, gate_v, up_v, sems = refs[14:]
    first = pltpu.make_async_copy(recv, recv_v, sems.at[10])
    first.start()
    copies = copies_of(gate_parts, gate_v, sems, 0) + copies_of(up_parts, up_v, sems, 5)
    for copy in copies:
        copy.start()
    order = packing(info[0], False)
    first.wait()
    unpack(recv_v, order, rows)
    for copy in copies:
        copy.wait()
    pre_gate = jnp.zeros((ROWS, HID), F32)
    pre_up = jnp.zeros((ROWS, HID), F32)
    for k in range(SHARDS):
        x = rows[:, k * WIDE : (k + 1) * WIDE]
        pre_gate += jnp.dot(x, gate_v[k], preferred_element_type=F32)
        pre_up += jnp.dot(x, up_v[k], preferred_element_type=F32)
    sigma = jax.nn.sigmoid(pre_gate)
    silu = pre_gate * sigma
    live = iota((ROWS, HID), 1) < info[1]
    hidden[...] = jnp.where(live, silu * pre_up, 0.0).astype(BF)
    slope_gate[...] = jnp.where(live, pre_up * sigma * (1.0 + pre_gate * (1.0 - sigma)), 0.0)
    slope_up[...] = jnp.where(live, silu, 0.0)


NT = (((1,), (1,)), ((), ()))


def backward_kernel(info, recv, slope_gate, slope_up, *refs):
    parts = refs[0:5]
    rows, d_gate, d_up = refs[5:8]
    recv_v, down_v, sems = refs[8:]
    first = pltpu.make_async_copy(recv, recv_v, sems.at[5])
    first.start()
    copies = copies_of(parts, down_v, sems, 0)
    for copy in copies:
        copy.start()
    order = packing(info[0], False)
    first.wait()
    unpack(recv_v, order, rows)
    for copy in copies:
        copy.wait()
    grad = jnp.zeros((ROWS, HID), F32)
    for k in range(SHARDS):
        grad += lax.dot_general(
            rows[:, k * WIDE : (k + 1) * WIDE], down_v[k], NT, preferred_element_type=F32
        )
    d_gate[...] = (grad * slope_gate[...]).astype(BF)
    d_up[...] = (grad * slope_up[...]).astype(BF)


def rows_kernel(info, d_gate, d_up, *refs):
    gate_parts, up_parts = refs[0:5], refs[5:10]
    send = refs[10]
    gate_v, up_v, held, sems = refs[11:]
    copies = copies_of(gate_parts, gate_v, sems, 0), copies_of(up_parts, up_v, sems, 5)
    for n in range(5):
        copies[0][n].start()
        copies[1][n].start()
    back = packing(info[0], True)
    for k, which in ((0, (0,)), (1, (1,)), (3, (2,)), (2, (3, 4))):
        for n in which:
            copies[0][n].wait()
            copies[1][n].wait()
        part = (
            lax.dot_general(d_gate[...], gate_v[k], NT, preferred_element_type=F32)
            + lax.dot_general(d_up[...], up_v[k], NT, preferred_element_type=F32)
        ).astype(BF)
        for n in range(2 * PIECES):
            held[n * 256 + k * 64 : n * 256 + k * 64 + 64, :] = part[n * 64 : n * 64 + 64, :]
    for piece in range(PIECES):
        for half in range(2):
            start = (piece * 2 + half) * 256
            send[half * 256 : half * 256 + 256, piece * WIDE : (piece + 1) * WIDE] = jnp.dot(
                back, held[start : start + 256, :], preferred_element_type=F32
            ).astype(BF)


RIGHT = [(n, (n + 1) % SHARDS) for n in range(SHARDS)]
LEFT = [(n, (n - 1) % SHARDS) for n in range(SHARDS)]


def to_right(x):
    return lax.ppermute(x, "dp", RIGHT)


def to_left(x):
    return lax.ppermute(x, "dp", LEFT)


def gather(own):
    half = own.shape[0] // 2
    left = to_right(own)
    right = to_left(own)
    opp_a = to_right(left[:half])
    opp_b = to_left(right[half:])
    return own, right, opp_a, opp_b, left


def scatter(own, right, opp, left):
    half = opp.shape[0] // 2
    narrow = lambda v: v.astype(BF)
    wide = lambda v: v.astype(F32)
    from_left = to_right(narrow(opp[:half]))
    from_right = to_left(narrow(opp[half:]))
    left_b = to_right(narrow(right[half:]))
    right_a = to_left(narrow(left[:half]))
    left_a = to_right(narrow(right[:half] + wide(from_left)))
    right_b = to_left(narrow(left[half:] + wide(from_right)))
    top = narrow(own[:half] + wide(left_a) + wide(right_a))
    bottom = narrow(own[half:] + wide(left_b) + wide(right_b))
    return jnp.concatenate([top, bottom], axis=0)


def exchange(x):
    return lax.all_to_all(
        x.reshape(CORES, 8, PIECES * WIDE), "expert", split_axis=0, concat_axis=0, tiled=True
    ).reshape(PACKED, PIECES * WIDE)


def on_device(tokens, cotangent, expert_ids, gates, widths, placement, w_gate, w_up, w_down):
    params = pltpu.CompilerParams(vmem_limit_bytes=LIMIT)
    experts = jnp.arange(CORES, dtype=jnp.int32)
    gate_parts = gather(w_gate[0])
    up_parts = gather(w_up[0])
    down_parts = gather(w_down[0])

    piece_rows = pl.BlockSpec((PACKED, TOK), lambda p: (p, 0))
    piece_cols = pl.BlockSpec((PACKED, WIDE), lambda p: (0, p))
    whole = lambda shape: pl.BlockSpec(shape, lambda p: (0, 0))
    packed_type = jax.ShapeDtypeStruct((PACKED, PIECES * WIDE), BF)
    map_type = jax.ShapeDtypeStruct((PIECES * PACKED, TOK), BF)
    send_x, move, scale = pl.pallas_call(
        route_kernel,
        grid=(PIECES,),
        in_specs=[
            whole((2, TOK)),
            whole((2, TOK)),
            whole((1, CORES)),
            whole((TOK, SHARDS * WIDE)),
        ],
        out_specs=[piece_cols, piece_rows, piece_rows],
        out_shape=[packed_type, map_type, map_type],
        scratch_shapes=[pltpu.VMEM((PACKED, TOK), F32)] * 3 + [pltpu.VMEM((PACKED, WIDE), BF)],
        compiler_params=params,
        cost_estimate=cost(1_700_000_000, 5_000_000),
        name="route",
    )(expert_ids.T, gates.astype(F32).T, placement[None], tokens)
    recv_x = exchange(send_x)
    send_g = pl.pallas_call(
        send_kernel,
        grid=(PIECES,),
        in_specs=[piece_rows, whole((TOK, SHARDS * WIDE))],
        out_specs=piece_cols,
        out_shape=packed_type,
        scratch_shapes=[pltpu.VMEM((PACKED, WIDE), BF)],
        compiler_params=params,
        cost_estimate=cost(1_700_000_000, 5_000_000),
        name="scale",
    )(scale, cotangent)
    recv_g = exchange(send_g)

    owner = jnp.sum(jnp.where(placement == lax.axis_index("expert"), experts, 0))
    width = jnp.sum(jnp.where(experts == owner, widths, 0))
    info = jnp.stack([lax.axis_index("dp").astype(jnp.int32), width])

    rows_type = jax.ShapeDtypeStruct((ROWS, SHARDS * WIDE), BF)
    hid_bf = jax.ShapeDtypeStruct((ROWS, HID), BF)
    hid_f32 = jax.ShapeDtypeStruct((ROWS, HID), F32)
    weight = pltpu.VMEM((SHARDS, WIDE, HID), BF)
    rows_x, hidden, slope_gate, slope_up = pl.pallas_call(
        forward_kernel,
        in_specs=[SMEM] + [ANY] * 11,
        out_specs=[VMEM] * 4,
        out_shape=[rows_type, hid_bf, hid_f32, hid_f32],
        scratch_shapes=[
            pltpu.VMEM((PACKED, PIECES * WIDE), BF),
            weight,
            weight,
            pltpu.SemaphoreType.DMA((11,)),
        ],
        compiler_params=params,
        cost_estimate=cost(4_000_000_000, 18_000_000),
        name="forward",
    )(info, recv_x, *gate_parts, *up_parts)
    rows_g, d_gate, d_up = pl.pallas_call(
        backward_kernel,
        in_specs=[SMEM, ANY, VMEM, VMEM] + [ANY] * 5,
        out_specs=[VMEM] * 3,
        out_shape=[rows_type, hid_bf, hid_bf],
        scratch_shapes=[
            pltpu.VMEM((PACKED, PIECES * WIDE), BF),
            pltpu.VMEM((SHARDS, HID, WIDE), BF),
            pltpu.SemaphoreType.DMA((6,)),
        ],
        compiler_params=params,
        cost_estimate=cost(2_400_000_000, 13_000_000),
        name="backward",
    )(info, recv_g, slope_gate, slope_up, *down_parts)
    send_d = pl.pallas_call(
        rows_kernel,
        in_specs=[SMEM, VMEM, VMEM] + [ANY] * 10,
        out_specs=VMEM,
        out_shape=packed_type,
        scratch_shapes=[
            weight,
            weight,
            pltpu.VMEM((2 * PIECES * 256, WIDE), BF),
            pltpu.SemaphoreType.DMA((10,)),
        ],
        compiler_params=params,
        cost_estimate=cost(4_000_000_000, 12_000_000),
        name="rows",
    )(info, d_gate, d_up, *gate_parts, *up_parts)
    recv_d = exchange(send_d)

    def block(x, k):
        return x[:, k * WIDE : (k + 1) * WIDE]

    dot = functools.partial(jnp.einsum, "ra,rb->ab", preferred_element_type=F32)
    grad_gate = scatter(*[dot(block(rows_x, k), d_gate) for k in range(SHARDS)])
    grad_up = scatter(*[dot(block(rows_x, k), d_up) for k in range(SHARDS)])
    grad_down = scatter(*[dot(hidden, block(rows_g, k)) for k in range(SHARDS)])

    grad_tokens = pl.pallas_call(
        combine_kernel,
        grid=(PIECES,),
        in_specs=[piece_rows, piece_cols],
        out_specs=whole((TOK, SHARDS * WIDE)),
        out_shape=jax.ShapeDtypeStruct((TOK, SHARDS * WIDE), BF),
        scratch_shapes=[pltpu.VMEM((PACKED, WIDE), F32)],
        compiler_params=params,
        cost_estimate=cost(1_700_000_000, 5_000_000),
        name="combine",
    )(move, recv_d)
    return (grad_tokens, grad_gate[None], grad_up[None], grad_down[None])


def solution(mesh):
    placed = (
        P(("dp", "expert"), None),
        P(("dp", "expert"), None),
        P(("dp", "expert"), None),
        P(("dp", "expert"), None),
        P(),
        P(),
        P("expert", "dp", None),
        P("expert", "dp", None),
        P("expert", None, "dp"),
    )
    return jax.shard_map(
        on_device,
        mesh=mesh,
        in_specs=placed,
        out_specs=(
            P(("dp", "expert"), None),
            P("expert", "dp", None),
            P("expert", "dp", None),
            P("expert", None, "dp"),
        ),
        check_vma=False,
    )
```

```python
import functools

import jax
import jax.numpy as jnp
from jax import lax
from jax.experimental import pallas as pl
from jax.experimental.pallas import tpu as pltpu
from jax.sharding import PartitionSpec as P

BF = jnp.bfloat16
F32 = jnp.float32
SHARDS = 4
SLOTS = 6
PIECES = 3
CORES = 64
TOK = 128
WIDE = 1024
HID = 512
ROWS = CORES * SLOTS
PACKED = CORES * 8
VMEM = pl.BlockSpec(memory_space=pltpu.VMEM)
SMEM = pl.BlockSpec(memory_space=pltpu.SMEM)
ANY = pl.BlockSpec(memory_space=pl.ANY)
LIMIT = 62 * 1024 * 1024


def iota(shape, dim):
    return lax.broadcasted_iota(jnp.int32, shape, dim)


def cost(flops, nbytes):
    return pl.CostEstimate(flops=flops, bytes_accessed=nbytes, transcendentals=0)


def spread(rows):
    chunk = (iota((PACKED, TOK), 0) % 8) // 2
    return jnp.concatenate(
        [jnp.where(chunk == c, rows, 0.0).astype(BF) for c in range(SHARDS)], axis=1
    )


def spread_turned(rows):
    chunk = (iota((TOK, PACKED), 1) % 8) // 2
    return jnp.concatenate(
        [jnp.where(chunk == c, rows, 0.0).astype(BF) for c in range(SHARDS)], axis=0
    )


def stacked(ref):
    return jnp.concatenate([ref[:, c * WIDE : (c + 1) * WIDE] for c in range(SHARDS)], axis=0)


def routing(ids, place):
    expert = iota((CORES, TOK), 0)
    slot_of = (iota((CORES, CORES), 0) == place[0:1, :]).astype(BF)
    hot = [
        jnp.dot(slot_of, (ids[k : k + 1, :] == expert).astype(BF), preferred_element_type=F32)
        for k in range(2)
    ]
    before = (iota((TOK, TOK), 0) < iota((TOK, TOK), 1)).astype(BF)
    count = jnp.dot((hot[0] + hot[1]).astype(BF), before, preferred_element_type=F32)
    return hot, count


def eightfold(x):
    return jnp.broadcast_to(x[:, None, :], (CORES, 8, TOK)).reshape(PACKED, TOK)


def slot_here(count, piece):
    return count == (2 * piece + iota((PACKED, TOK), 0) % 2).astype(F32)


def route_kernel(ids, place, tok, send, hot_s, count_s, tok_s):
    piece = pl.program_id(0)

    @pl.when(piece == 0)
    def _():
        hot, count = routing(ids, place)
        hot_s[...] = eightfold(hot[0] + hot[1])
        count_s[...] = eightfold(count)
        tok_s[...] = stacked(tok)

    rows = jnp.where(slot_here(count_s[...], piece), hot_s[...], 0.0)
    send[...] = jnp.dot(spread(rows), tok_s[...], preferred_element_type=F32).astype(BF)


def scale_kernel(ids, place, gates, cot, send, turned, hot_s, count_s, gate_s, cot_s):
    piece = pl.program_id(0)

    @pl.when(piece == 0)
    def _():
        hot, count = routing(ids, place)
        hot_s[...] = eightfold(hot[0] + hot[1])
        count_s[...] = eightfold(count)
        gate_s[...] = eightfold(hot[0] * gates[0:1, :] + hot[1] * gates[1:2, :])
        cot_s[...] = stacked(cot)

    here = slot_here(count_s[...], piece)
    rows = jnp.where(here, gate_s[...], 0.0)
    send[...] = jnp.dot(spread(rows), cot_s[...], preferred_element_type=F32).astype(BF)
    turned[...] = spread_turned(jnp.where(here, hot_s[...], 0.0).T)


def combine_kernel(turned, back, out, acc):
    piece = pl.program_id(0)
    part = jnp.dot(turned[...], back[...], preferred_element_type=F32)

    @pl.when(piece == 0)
    def _():
        acc[...] = part

    @pl.when(piece == 1)
    def _():
        acc[...] += part

    @pl.when(piece == PIECES - 1)
    def _():
        total = (acc[...] + part).astype(BF)
        for c in range(SHARDS):
            out[:, c * WIDE : (c + 1) * WIDE] = total[c * TOK : (c + 1) * TOK, :]


def packing(member, turned):
    shape = (256, 256)
    outer, inner = iota(shape, 1 if turned else 0), iota(shape, 0 if turned else 1)
    within = outer % 64
    chunk = (member + outer // 64) % SHARDS
    return (inner == (within // 2) * 8 + chunk * 2 + within % 2).astype(BF)


def unpack(packed, order, blocks):
    for piece in range(PIECES):
        for half in range(2):
            block = jnp.dot(
                order,
                packed[half * 256 : half * 256 + 256, piece * WIDE : (piece + 1) * WIDE],
                preferred_element_type=F32,
            ).astype(BF)
            start = (piece * 2 + half) * 64
            for k in range(SHARDS):
                blocks[k][start : start + 64, :] = block[k * 64 : k * 64 + 64, :]


def copies_of(parts, dest, sems, base):
    own, right, opp_a, opp_b, left = parts
    half = opp_a.shape[0]
    pairs = (
        (own, dest.at[0]),
        (right, dest.at[1]),
        (opp_a, dest.at[2, pl.ds(0, half)]),
        (opp_b, dest.at[2, pl.ds(half, half)]),
        (left, dest.at[3]),
    )
    return [pltpu.make_async_copy(s, d, sems.at[base + n]) for n, (s, d) in enumerate(pairs)]


def begin(copies):
    for copy in copies:
        copy.start()


def finish(copies):
    for copy in copies:
        copy.wait()


def forward_kernel(info, recv, *refs):
    gate_parts, up_parts = refs[0:5], refs[5:10]
    blocks = refs[10:14]
    hidden, slope_gate, slope_up = refs[14:17]
    recv_v, gate_v, up_v, sems = refs[17:]
    first = pltpu.make_async_copy(recv, recv_v, sems.at[10])
    first.start()
    copies = copies_of(gate_parts, gate_v, sems, 0) + copies_of(up_parts, up_v, sems, 5)
    begin(copies)
    order = packing(info[0], False)
    first.wait()
    unpack(recv_v, order, blocks)
    finish(copies)
    pre_gate = jnp.zeros((ROWS, HID), F32)
    pre_up = jnp.zeros((ROWS, HID), F32)
    for k in range(SHARDS):
        x = blocks[k][...]
        pre_gate += jnp.dot(x, gate_v[k], preferred_element_type=F32)
        pre_up += jnp.dot(x, up_v[k], preferred_element_type=F32)
    sigma = jax.nn.sigmoid(pre_gate)
    silu = pre_gate * sigma
    live = iota((ROWS, HID), 1) < info[1]
    hidden[...] = jnp.where(live, silu * pre_up, 0.0).astype(BF)
    slope_gate[...] = jnp.where(live, pre_up * sigma * (1.0 + pre_gate * (1.0 - sigma)), 0.0)
    slope_up[...] = jnp.where(live, silu, 0.0)


NT = (((1,), (1,)), ((), ()))


def backward_kernel(info, recv, slope_gate, slope_up, *refs):
    down_parts, gate_parts, up_parts = refs[0:5], refs[5:10], refs[10:15]
    rows_out = refs[15:19]
    d_gate, d_up, send = refs[19:22]
    recv_v, slope_gate_v, slope_up_v, down_v, gate_v, up_v = refs[22:28]
    blocks = refs[28:32]
    held, send_v, sems = refs[32:]
    first = pltpu.make_async_copy(recv, recv_v, sems.at[0])
    first.start()
    down = copies_of(down_parts, down_v, sems, 3)
    begin(down)
    slopes = [
        pltpu.make_async_copy(slope_gate, slope_gate_v, sems.at[1]),
        pltpu.make_async_copy(slope_up, slope_up_v, sems.at[2]),
    ]
    begin(slopes)
    wide = copies_of(gate_parts, gate_v, sems, 8) + copies_of(up_parts, up_v, sems, 13)
    begin(wide)
    order = packing(info[0], False)
    first.wait()
    unpack(recv_v, order, blocks)
    outs = [
        pltpu.make_async_copy(blocks[k], rows_out[k], sems.at[18 + k]) for k in range(SHARDS)
    ]
    begin(outs)
    finish(down)
    grad = jnp.zeros((ROWS, HID), F32)
    for k in range(SHARDS):
        grad += lax.dot_general(blocks[k][...], down_v[k], NT, preferred_element_type=F32)
    finish(slopes)
    d_gate[...] = (grad * slope_gate_v[...]).astype(BF)
    d_up[...] = (grad * slope_up_v[...]).astype(BF)
    finish(wide)
    for k in range(SHARDS):
        part = (
            lax.dot_general(d_gate[...], gate_v[k], NT, preferred_element_type=F32)
            + lax.dot_general(d_up[...], up_v[k], NT, preferred_element_type=F32)
        ).astype(BF)
        for n in range(2 * PIECES):
            held[n * 256 + k * 64 : n * 256 + k * 64 + 64, :] = part[n * 64 : n * 64 + 64, :]
    back = packing(info[0], True)
    for piece in range(PIECES):
        for half in range(2):
            start = (piece * 2 + half) * 256
            send_v[piece, half * 256 : half * 256 + 256, :] = jnp.dot(
                back, held[start : start + 256, :], preferred_element_type=F32
            ).astype(BF)
        copy = pltpu.make_async_copy(
            send_v.at[piece], send.at[:, pl.ds(piece * WIDE, WIDE)], sems.at[22 + piece]
        )
        copy.start()
        outs.append(copy)
    finish(outs)


RIGHT = [(n, (n + 1) % SHARDS) for n in range(SHARDS)]
LEFT = [(n, (n - 1) % SHARDS) for n in range(SHARDS)]


def to_right(x):
    return lax.ppermute(x, "dp", RIGHT)


def to_left(x):
    return lax.ppermute(x, "dp", LEFT)


def near(own):
    return to_right(own), to_left(own)


def far(left, right):
    half = left.shape[0] // 2
    return to_right(left[:half]), to_left(right[half:])


def scatter(own, right, opp, left):
    half = opp.shape[0] // 2
    narrow = lambda v: v.astype(BF)
    wide = lambda v: v.astype(F32)
    from_left = to_right(narrow(opp[:half]))
    from_right = to_left(narrow(opp[half:]))
    left_b = to_right(narrow(right[half:]))
    right_a = to_left(narrow(left[:half]))
    left_a = to_right(narrow(right[:half] + wide(from_left)))
    right_b = to_left(narrow(left[half:] + wide(from_right)))
    top = narrow(own[:half] + wide(left_a) + wide(right_a))
    bottom = narrow(own[half:] + wide(left_b) + wide(right_b))
    return jnp.concatenate([top, bottom], axis=0)


def exchange(x):
    return lax.all_to_all(
        x.reshape(CORES, 8, PIECES * WIDE), "expert", split_axis=0, concat_axis=0, tiled=True
    ).reshape(PACKED, PIECES * WIDE)


def on_device(tokens, cotangent, expert_ids, gates, widths, placement, w_gate, w_up, w_down):
    params = pltpu.CompilerParams(vmem_limit_bytes=LIMIT)
    experts = jnp.arange(CORES, dtype=jnp.int32)
    owner = jnp.sum(jnp.where(placement == lax.axis_index("expert"), experts, 0))
    width = jnp.sum(jnp.where(experts == owner, widths, 0))
    info = jnp.stack([lax.axis_index("dp").astype(jnp.int32), width])
    shards = (w_gate[0], w_up[0], w_down[0])
    nears = [near(w) for w in shards]

    turned_rows = pl.BlockSpec((PACKED, PACKED), lambda p: (p, 0))
    piece_cols = pl.BlockSpec((PACKED, WIDE), lambda p: (0, p))
    whole = lambda shape: pl.BlockSpec(shape, lambda p: (0, 0))
    small = [whole((2, TOK)), whole((1, CORES))]
    rowwise = whole((TOK, SHARDS * WIDE))
    packed_type = jax.ShapeDtypeStruct((PACKED, PIECES * WIDE), BF)
    mapped = pltpu.VMEM((PACKED, TOK), F32)
    tall = pltpu.VMEM((PACKED, WIDE), BF)
    ids = expert_ids.T
    place = placement[None]
    send_x = pl.pallas_call(
        route_kernel,
        grid=(PIECES,),
        in_specs=small + [rowwise],
        out_specs=piece_cols,
        out_shape=packed_type,
        scratch_shapes=[mapped, mapped, tall],
        compiler_params=params,
        cost_estimate=cost(1_700_000_000, 5_000_000),
        name="route",
    )(ids, place, tokens)
    recv_x = exchange(send_x)
    send_g, turned = pl.pallas_call(
        scale_kernel,
        grid=(PIECES,),
        in_specs=small + [whole((2, TOK)), rowwise],
        out_specs=[piece_cols, turned_rows],
        out_shape=[packed_type, jax.ShapeDtypeStruct((PIECES * PACKED, PACKED), BF)],
        scratch_shapes=[mapped, mapped, mapped, tall],
        compiler_params=params,
        cost_estimate=cost(1_700_000_000, 6_000_000),
        name="scale",
    )(ids, place, gates.astype(F32).T, cotangent)
    send_g, nears = lax.optimization_barrier((send_g, nears))
    recv_g = exchange(send_g)
    parts = []
    for own, (left, right) in zip(shards, nears):
        opp_a, opp_b = far(left, right)
        parts.append((own, right, opp_a, opp_b, left))
    gate_parts, up_parts, down_parts = parts

    block_type = jax.ShapeDtypeStruct((ROWS, WIDE), BF)
    hid_bf = jax.ShapeDtypeStruct((ROWS, HID), BF)
    hid_f32 = jax.ShapeDtypeStruct((ROWS, HID), F32)
    weight = pltpu.VMEM((SHARDS, WIDE, HID), BF)
    packed_v = pltpu.VMEM((PACKED, PIECES * WIDE), BF)
    block_v = pltpu.VMEM((ROWS, WIDE), BF)
    *blocks_x, hidden, slope_gate, slope_up = pl.pallas_call(
        forward_kernel,
        in_specs=[SMEM] + [ANY] * 11,
        out_specs=[VMEM] * 7,
        out_shape=[block_type] * 4 + [hid_bf, hid_f32, hid_f32],
        scratch_shapes=[packed_v, weight, weight, pltpu.SemaphoreType.DMA((11,))],
        compiler_params=params,
        cost_estimate=cost(4_000_000_000, 18_000_000),
        name="forward",
    )(info, recv_x, *gate_parts, *up_parts)

    mid = ROWS // 2
    x_left, x_right = to_right(blocks_x[1]), to_left(blocks_x[3])
    x_far = (
        to_right(to_right(blocks_x[2][:mid])),
        to_left(to_left(blocks_x[2][mid:])),
    )

    recv_g, x_left, x_right, x_far = lax.optimization_barrier((recv_g, x_left, x_right, x_far))

    *blocks_g, d_gate, d_up, send_d = pl.pallas_call(
        backward_kernel,
        in_specs=[SMEM] + [ANY] * 18,
        out_specs=[ANY] * 4 + [VMEM, VMEM, ANY],
        out_shape=[block_type] * 4 + [hid_bf, hid_bf, packed_type],
        scratch_shapes=[
            packed_v,
            pltpu.VMEM((ROWS, HID), F32),
            pltpu.VMEM((ROWS, HID), F32),
            pltpu.VMEM((SHARDS, HID, WIDE), BF),
            weight,
            weight,
            *[block_v] * 4,
            pltpu.VMEM((2 * PIECES * 256, WIDE), BF),
            pltpu.VMEM((PIECES, PACKED, WIDE), BF),
            pltpu.SemaphoreType.DMA((25,)),
        ],
        compiler_params=params,
        cost_estimate=cost(7_000_000_000, 26_000_000),
        name="backward",
    )(info, recv_g, slope_gate, slope_up, *down_parts, *gate_parts, *up_parts)
    recv_d = exchange(send_d)

    dot = functools.partial(jnp.einsum, "ra,rb->ab", preferred_element_type=F32)

    def summed(d):
        left, right = near(d)
        opp_a, opp_b = far(left, right)
        return (
            dot(blocks_x[0], d)
            + dot(x_left, left)
            + dot(x_right, right)
            + dot(x_far[0], opp_a)
            + dot(x_far[1], opp_b)
        ).astype(BF)

    grad_gate = summed(d_gate)
    grad_up = summed(d_up)
    grad_down = scatter(*[dot(hidden, block) for block in blocks_g])

    grad_tokens = pl.pallas_call(
        combine_kernel,
        grid=(PIECES,),
        in_specs=[turned_rows, piece_cols],
        out_specs=rowwise,
        out_shape=jax.ShapeDtypeStruct((TOK, SHARDS * WIDE), BF),
        scratch_shapes=[pltpu.VMEM((PACKED, WIDE), F32)],
        compiler_params=params,
        cost_estimate=cost(1_700_000_000, 5_000_000),
        name="combine",
    )(turned, recv_d)
    return (grad_tokens, grad_gate[None], grad_up[None], grad_down[None])


def solution(mesh):
    placed = (
        P(("dp", "expert"), None),
        P(("dp", "expert"), None),
        P(("dp", "expert"), None),
        P(("dp", "expert"), None),
        P(),
        P(),
        P("expert", "dp", None),
        P("expert", "dp", None),
        P("expert", None, "dp"),
    )
    return jax.shard_map(
        on_device,
        mesh=mesh,
        in_specs=placed,
        out_specs=(
            P(("dp", "expert"), None),
            P("expert", "dp", None),
            P("expert", "dp", None),
            P("expert", None, "dp"),
        ),
        check_vma=False,
    )
```

```python
import functools

import jax
import jax.numpy as jnp
from jax import lax
from jax.experimental import pallas as pl
from jax.experimental.pallas import tpu as pltpu
from jax.sharding import PartitionSpec as P

BF = jnp.bfloat16
F32 = jnp.float32
SHARDS = 4
SLOTS = 6
PIECES = 3
CORES = 64
TOK = 128
WIDE = 1024
HID = 512
ROWS = CORES * SLOTS
PACKED = CORES * 8
VMEM = pl.BlockSpec(memory_space=pltpu.VMEM)
SMEM = pl.BlockSpec(memory_space=pltpu.SMEM)
ANY = pl.BlockSpec(memory_space=pl.ANY)
LIMIT = 62 * 1024 * 1024


def iota(shape, dim):
    return lax.broadcasted_iota(jnp.int32, shape, dim)


def spread(rows):
    chunk = (iota((PACKED, TOK), 0) % 8) // 2
    return jnp.concatenate(
        [jnp.where(chunk == c, rows, 0.0).astype(BF) for c in range(SHARDS)], axis=1
    )


def spread_turned(rows):
    chunk = (iota((TOK, PACKED), 1) % 8) // 2
    return jnp.concatenate(
        [jnp.where(chunk == c, rows, 0.0).astype(BF) for c in range(SHARDS)], axis=0
    )


def stacked(ref):
    return jnp.concatenate([ref[:, c * WIDE : (c + 1) * WIDE] for c in range(SHARDS)], axis=0)


def routing(ids, place):
    expert = iota((CORES, TOK), 0)
    slot_of = (iota((CORES, CORES), 0) == place[0:1, :]).astype(BF)
    hot = [
        jnp.dot(slot_of, (ids[k : k + 1, :] == expert).astype(BF), preferred_element_type=F32)
        for k in range(2)
    ]
    before = (iota((TOK, TOK), 0) < iota((TOK, TOK), 1)).astype(BF)
    count = jnp.dot((hot[0] + hot[1]).astype(BF), before, preferred_element_type=F32)
    return hot, count


def eightfold(x):
    return jnp.broadcast_to(x[:, None, :], (CORES, 8, TOK)).reshape(PACKED, TOK)


def slot_here(count, piece):
    return count == (2 * piece + iota((PACKED, TOK), 0) % 2).astype(F32)


def route_kernel(ids, place, tok, send, hot_s, count_s, tok_s):
    piece = pl.program_id(0)

    @pl.when(piece == 0)
    def _():
        hot, count = routing(ids, place)
        hot_s[...] = eightfold(hot[0] + hot[1])
        count_s[...] = eightfold(count)
        tok_s[...] = stacked(tok)

    rows = jnp.where(slot_here(count_s[...], piece), hot_s[...], 0.0)
    send[...] = jnp.dot(spread(rows), tok_s[...], preferred_element_type=F32).astype(BF)


def scale_kernel(ids, place, gates, cot, send, turned, hot_s, count_s, gate_s, cot_s):
    piece = pl.program_id(0)

    @pl.when(piece == 0)
    def _():
        hot, count = routing(ids, place)
        hot_s[...] = eightfold(hot[0] + hot[1])
        count_s[...] = eightfold(count)
        gate_s[...] = eightfold(hot[0] * gates[0:1, :] + hot[1] * gates[1:2, :])
        cot_s[...] = stacked(cot)

    here = slot_here(count_s[...], piece)
    rows = jnp.where(here, gate_s[...], 0.0)
    send[...] = jnp.dot(spread(rows), cot_s[...], preferred_element_type=F32).astype(BF)
    turned[...] = spread_turned(jnp.where(here, hot_s[...], 0.0).T)


def combine_kernel(turned, back, out, acc):
    piece = pl.program_id(0)
    part = jnp.dot(turned[...], back[...], preferred_element_type=F32)

    @pl.when(piece == 0)
    def _():
        acc[...] = part

    @pl.when(piece == 1)
    def _():
        acc[...] += part

    @pl.when(piece == PIECES - 1)
    def _():
        total = (acc[...] + part).astype(BF)
        for c in range(SHARDS):
            out[:, c * WIDE : (c + 1) * WIDE] = total[c * TOK : (c + 1) * TOK, :]


def packing(member, turned):
    shape = (256, 256)
    outer, inner = iota(shape, 1 if turned else 0), iota(shape, 0 if turned else 1)
    within = outer % 64
    chunk = (member + outer // 64) % SHARDS
    return (inner == (within // 2) * 8 + chunk * 2 + within % 2).astype(BF)


def unpack(packed, order, blocks):
    for piece in range(PIECES):
        for half in range(2):
            block = jnp.dot(
                order,
                packed[half * 256 : half * 256 + 256, piece * WIDE : (piece + 1) * WIDE],
                preferred_element_type=F32,
            ).astype(BF)
            start = (piece * 2 + half) * 64
            for k in range(SHARDS):
                blocks[k][start : start + 64, :] = block[k * 64 : k * 64 + 64, :]


def copies_of(parts, dest, sems, base):
    own, right, opp_a, opp_b, left = parts
    half = opp_a.shape[0]
    pairs = (
        (own, dest.at[0]),
        (right, dest.at[1]),
        (opp_a, dest.at[2, pl.ds(0, half)]),
        (opp_b, dest.at[2, pl.ds(half, half)]),
        (left, dest.at[3]),
    )
    return [pltpu.make_async_copy(s, d, sems.at[base + n]) for n, (s, d) in enumerate(pairs)]


def begin(copies):
    for copy in copies:
        copy.start()


def finish(copies):
    for copy in copies:
        copy.wait()


def unpack_kernel(info, recv, *blocks):
    unpack(recv, packing(info[0], False), blocks)


def forward_kernel(info, *refs):
    blocks = refs[0:4]
    gate_parts, up_parts = refs[4:9], refs[9:14]
    hidden, slope_gate, slope_up = refs[14:17]
    gate_v, up_v, sems = refs[17:]
    copies = copies_of(gate_parts, gate_v, sems, 0) + copies_of(up_parts, up_v, sems, 5)
    begin(copies)
    finish(copies)
    pre_gate = jnp.zeros((ROWS, HID), F32)
    pre_up = jnp.zeros((ROWS, HID), F32)
    for k in range(SHARDS):
        x = blocks[k][...]
        pre_gate += jnp.dot(x, gate_v[k], preferred_element_type=F32)
        pre_up += jnp.dot(x, up_v[k], preferred_element_type=F32)
    sigma = jax.nn.sigmoid(pre_gate)
    silu = pre_gate * sigma
    live = iota((ROWS, HID), 1) < info[1]
    hidden[...] = jnp.where(live, silu * pre_up, 0.0).astype(BF)
    slope_gate[...] = jnp.where(live, pre_up * sigma * (1.0 + pre_gate * (1.0 - sigma)), 0.0)
    slope_up[...] = jnp.where(live, silu, 0.0)


NT = (((1,), (1,)), ((), ()))


def backward_kernel(info, recv, slope_gate, slope_up, *refs):
    down_parts, gate_parts, up_parts = refs[0:5], refs[5:10], refs[10:15]
    rows_out = refs[15:19]
    d_gate, d_up, send = refs[19:22]
    recv_v, slope_gate_v, slope_up_v, down_v, gate_v, up_v = refs[22:28]
    blocks = refs[28:32]
    held, send_v, sems = refs[32:]
    first = pltpu.make_async_copy(recv, recv_v, sems.at[0])
    first.start()
    down = copies_of(down_parts, down_v, sems, 3)
    begin(down)
    slopes = [
        pltpu.make_async_copy(slope_gate, slope_gate_v, sems.at[1]),
        pltpu.make_async_copy(slope_up, slope_up_v, sems.at[2]),
    ]
    begin(slopes)
    wide = copies_of(gate_parts, gate_v, sems, 8) + copies_of(up_parts, up_v, sems, 13)
    begin(wide)
    order = packing(info[0], False)
    first.wait()
    unpack(recv_v, order, blocks)
    outs = [
        pltpu.make_async_copy(blocks[k], rows_out[k], sems.at[18 + k]) for k in range(SHARDS)
    ]
    begin(outs)
    finish(down)
    grad = jnp.zeros((ROWS, HID), F32)
    for k in range(SHARDS):
        grad += lax.dot_general(blocks[k][...], down_v[k], NT, preferred_element_type=F32)
    finish(slopes)
    d_gate[...] = (grad * slope_gate_v[...]).astype(BF)
    d_up[...] = (grad * slope_up_v[...]).astype(BF)
    finish(wide)
    for k in range(SHARDS):
        part = (
            lax.dot_general(d_gate[...], gate_v[k], NT, preferred_element_type=F32)
            + lax.dot_general(d_up[...], up_v[k], NT, preferred_element_type=F32)
        ).astype(BF)
        for n in range(2 * PIECES):
            held[n * 256 + k * 64 : n * 256 + k * 64 + 64, :] = part[n * 64 : n * 64 + 64, :]
    back = packing(info[0], True)
    for piece in range(PIECES):
        for half in range(2):
            start = (piece * 2 + half) * 256
            send_v[piece, half * 256 : half * 256 + 256, :] = jnp.dot(
                back, held[start : start + 256, :], preferred_element_type=F32
            ).astype(BF)
        copy = pltpu.make_async_copy(
            send_v.at[piece], send.at[:, pl.ds(piece * WIDE, WIDE)], sems.at[22 + piece]
        )
        copy.start()
        outs.append(copy)
    finish(outs)


RIGHT = [(n, (n + 1) % SHARDS) for n in range(SHARDS)]
LEFT = [(n, (n - 1) % SHARDS) for n in range(SHARDS)]


def to_right(x):
    return lax.ppermute(x, "dp", RIGHT)


def to_left(x):
    return lax.ppermute(x, "dp", LEFT)


def near(own):
    return to_right(own), to_left(own)


def far(left, right):
    half = left.shape[0] // 2
    return to_right(left[:half]), to_left(right[half:])


def scatter(own, right, opp, left):
    half = opp.shape[0] // 2
    narrow = lambda v: v.astype(BF)
    wide = lambda v: v.astype(F32)
    from_left = to_right(narrow(opp[:half]))
    from_right = to_left(narrow(opp[half:]))
    left_b = to_right(narrow(right[half:]))
    right_a = to_left(narrow(left[:half]))
    left_a = to_right(narrow(right[:half] + wide(from_left)))
    right_b = to_left(narrow(left[half:] + wide(from_right)))
    top = narrow(own[:half] + wide(left_a) + wide(right_a))
    bottom = narrow(own[half:] + wide(left_b) + wide(right_b))
    return jnp.concatenate([top, bottom], axis=0)


def exchange(x):
    return lax.all_to_all(
        x.reshape(CORES, 8, PIECES * WIDE), "expert", split_axis=0, concat_axis=0, tiled=True
    ).reshape(PACKED, PIECES * WIDE)


PARAMS = pltpu.CompilerParams(vmem_limit_bytes=LIMIT)
PACKED_TYPE = jax.ShapeDtypeStruct((PACKED, PIECES * WIDE), BF)
BLOCK_TYPE = jax.ShapeDtypeStruct((ROWS, WIDE), BF)
HID_BF = jax.ShapeDtypeStruct((ROWS, HID), BF)
HID_F32 = jax.ShapeDtypeStruct((ROWS, HID), F32)
WEIGHT = pltpu.VMEM((SHARDS, WIDE, HID), BF)
PACKED_V = pltpu.VMEM((PACKED, PIECES * WIDE), BF)
MAPPED = pltpu.VMEM((PACKED, TOK), F32)
TALL = pltpu.VMEM((PACKED, WIDE), BF)
TURNED_ROWS = pl.BlockSpec((PACKED, PACKED), lambda p: (p, 0))
PIECE_COLS = pl.BlockSpec((PACKED, WIDE), lambda p: (0, p))


def whole(*shape):
    return pl.BlockSpec(shape, lambda p: (0, 0))


def call(kernel, flops, nbytes, name, **rest):
    estimate = pl.CostEstimate(flops=flops, bytes_accessed=nbytes, transcendentals=0)
    return pl.pallas_call(
        kernel, compiler_params=PARAMS, cost_estimate=estimate, name=name, **rest
    )


def run_route(ids, place, tokens):
    return call(
        route_kernel, 1_700_000_000, 5_000_000, "route",
        grid=(PIECES,),
        in_specs=[whole(2, TOK), whole(1, CORES), whole(TOK, SHARDS * WIDE)],
        out_specs=PIECE_COLS,
        out_shape=PACKED_TYPE,
        scratch_shapes=[MAPPED, MAPPED, TALL],
    )(ids, place, tokens)


def run_scale(ids, place, gates, cotangent):
    return call(
        scale_kernel, 1_700_000_000, 6_000_000, "scale",
        grid=(PIECES,),
        in_specs=[whole(2, TOK), whole(1, CORES), whole(2, TOK), whole(TOK, SHARDS * WIDE)],
        out_specs=[PIECE_COLS, TURNED_ROWS],
        out_shape=[PACKED_TYPE, jax.ShapeDtypeStruct((PIECES * PACKED, PACKED), BF)],
        scratch_shapes=[MAPPED, MAPPED, MAPPED, TALL],
    )(ids, place, gates, cotangent)


def run_unpack(info, recv):
    return call(
        unpack_kernel, 800_000_000, 6_000_000, "unpack",
        in_specs=[SMEM, VMEM],
        out_specs=[VMEM] * 4,
        out_shape=[BLOCK_TYPE] * 4,
    )(info, recv)


def run_forward(info, blocks, gate_parts, up_parts):
    return call(
        forward_kernel, 3_300_000_000, 14_000_000, "forward",
        in_specs=[SMEM] + [VMEM] * 4 + [ANY] * 10,
        out_specs=[VMEM] * 3,
        out_shape=[HID_BF, HID_F32, HID_F32],
        scratch_shapes=[WEIGHT, WEIGHT, pltpu.SemaphoreType.DMA((10,))],
    )(info, *blocks, *gate_parts, *up_parts)


def run_backward(info, recv, slope_gate, slope_up, down_parts, gate_parts, up_parts):
    return call(
        backward_kernel, 7_000_000_000, 26_000_000, "backward",
        in_specs=[SMEM] + [ANY] * 18,
        out_specs=[ANY] * 4 + [VMEM, VMEM, ANY],
        out_shape=[BLOCK_TYPE] * 4 + [HID_BF, HID_BF, PACKED_TYPE],
        scratch_shapes=[
            PACKED_V,
            pltpu.VMEM((ROWS, HID), F32),
            pltpu.VMEM((ROWS, HID), F32),
            pltpu.VMEM((SHARDS, HID, WIDE), BF),
            WEIGHT,
            WEIGHT,
            *[pltpu.VMEM((ROWS, WIDE), BF)] * 4,
            pltpu.VMEM((2 * PIECES * 256, WIDE), BF),
            pltpu.VMEM((PIECES, PACKED, WIDE), BF),
            pltpu.SemaphoreType.DMA((25,)),
        ],
    )(info, recv, slope_gate, slope_up, *down_parts, *gate_parts, *up_parts)


def run_combine(turned, recv):
    return call(
        combine_kernel, 1_700_000_000, 5_000_000, "combine",
        grid=(PIECES,),
        in_specs=[TURNED_ROWS, PIECE_COLS],
        out_specs=whole(TOK, SHARDS * WIDE),
        out_shape=jax.ShapeDtypeStruct((TOK, SHARDS * WIDE), BF),
        scratch_shapes=[pltpu.VMEM((PACKED, WIDE), F32)],
    )(turned, recv)


def on_device(tokens, cotangent, expert_ids, gates, widths, placement, w_gate, w_up, w_down):
    experts = jnp.arange(CORES, dtype=jnp.int32)
    owner = jnp.sum(jnp.where(placement == lax.axis_index("expert"), experts, 0))
    width = jnp.sum(jnp.where(experts == owner, widths, 0))
    info = jnp.stack([lax.axis_index("dp").astype(jnp.int32), width])
    shards = (w_gate[0], w_up[0], w_down[0])
    nears = [near(w) for w in shards]
    ids = expert_ids.T
    place = placement[None]

    recv_x = exchange(run_route(ids, place, tokens))
    send_g, turned = run_scale(ids, place, gates.astype(F32).T, cotangent)
    send_g, nears, info = lax.optimization_barrier((send_g, nears, info))
    recv_g = exchange(send_g)
    parts = []
    for own, (left, right) in zip(shards, nears):
        opp_a, opp_b = far(left, right)
        parts.append((own, right, opp_a, opp_b, left))
    gate_parts, up_parts, down_parts = parts

    blocks_x = run_unpack(info, recv_x)
    mid = ROWS // 2
    x_left, x_right = to_right(blocks_x[1]), to_left(blocks_x[3])
    x_passing = to_right(blocks_x[2][:mid]), to_left(blocks_x[2][mid:])

    hidden, slope_gate, slope_up = run_forward(info, blocks_x, gate_parts, up_parts)
    recv_g, x_left, x_right, x_passing = lax.optimization_barrier(
        (recv_g, x_left, x_right, x_passing)
    )
    x_far = to_right(x_passing[0]), to_left(x_passing[1])

    *blocks_g, d_gate, d_up, send_d = run_backward(
        info, recv_g, slope_gate, slope_up, down_parts, gate_parts, up_parts
    )
    recv_d = exchange(send_d)

    dot = functools.partial(jnp.einsum, "ra,rb->ab", preferred_element_type=F32)

    def summed(d):
        left, right = near(d)
        opp_a, opp_b = far(left, right)
        return (
            dot(blocks_x[0], d)
            + dot(x_left, left)
            + dot(x_right, right)
            + dot(x_far[0], opp_a)
            + dot(x_far[1], opp_b)
        ).astype(BF)

    grad_gate = summed(d_gate)
    grad_up = summed(d_up)
    grad_down = scatter(*[dot(hidden, block) for block in blocks_g])
    grad_tokens = run_combine(turned, recv_d)
    return (grad_tokens, grad_gate[None], grad_up[None], grad_down[None])


def solution(mesh):
    placed = (
        P(("dp", "expert"), None),
        P(("dp", "expert"), None),
        P(("dp", "expert"), None),
        P(("dp", "expert"), None),
        P(),
        P(),
        P("expert", "dp", None),
        P("expert", "dp", None),
        P("expert", None, "dp"),
    )
    return jax.shard_map(
        on_device,
        mesh=mesh,
        in_specs=placed,
        out_specs=(
            P(("dp", "expert"), None),
            P("expert", "dp", None),
            P("expert", "dp", None),
            P("expert", None, "dp"),
        ),
        check_vma=False,
    )
```

```python
import functools

import jax
import jax.numpy as jnp
from jax import lax
from jax.experimental import pallas as pl
from jax.experimental.pallas import tpu as pltpu
from jax.sharding import PartitionSpec as P

BF = jnp.bfloat16
F32 = jnp.float32
SHARDS = 4
SLOTS = 6
PIECES = 3
CORES = 64
TOK = 128
WIDE = 1024
HID = 512
ROWS = CORES * SLOTS
PACKED = CORES * 8
VMEM = pl.BlockSpec(memory_space=pltpu.VMEM)
SMEM = pl.BlockSpec(memory_space=pltpu.SMEM)
ANY = pl.BlockSpec(memory_space=pl.ANY)
MIB = 1024 * 1024


def iota(shape, dim):
    return lax.broadcasted_iota(jnp.int32, shape, dim)


def spread(rows):
    chunk = (iota((PACKED, TOK), 0) % 8) // 2
    return jnp.concatenate(
        [jnp.where(chunk == c, rows, 0.0).astype(BF) for c in range(SHARDS)], axis=1
    )


def spread_turned(rows):
    chunk = (iota((TOK, PACKED), 1) % 8) // 2
    return jnp.concatenate(
        [jnp.where(chunk == c, rows, 0.0).astype(BF) for c in range(SHARDS)], axis=0
    )


def stacked(ref):
    return jnp.concatenate([ref[:, c * WIDE : (c + 1) * WIDE] for c in range(SHARDS)], axis=0)


def routing(ids, place):
    expert = iota((CORES, TOK), 0)
    slot_of = (iota((CORES, CORES), 0) == place[0:1, :]).astype(BF)
    hot = [
        jnp.dot(slot_of, (ids[k : k + 1, :] == expert).astype(BF), preferred_element_type=F32)
        for k in range(2)
    ]
    before = (iota((TOK, TOK), 0) < iota((TOK, TOK), 1)).astype(BF)
    count = jnp.dot((hot[0] + hot[1]).astype(BF), before, preferred_element_type=F32)
    return hot, count


def eightfold(x):
    return jnp.broadcast_to(x[:, None, :], (CORES, 8, TOK)).reshape(PACKED, TOK)


def slot_here(count, piece):
    return count == (2 * piece + iota((PACKED, TOK), 0) % 2).astype(F32)


def route_kernel(ids, place, tok, send, hot_s, count_s, tok_s):
    piece = pl.program_id(0)

    @pl.when(piece == 0)
    def _():
        hot, count = routing(ids, place)
        hot_s[...] = eightfold(hot[0] + hot[1])
        count_s[...] = eightfold(count)
        tok_s[...] = stacked(tok)

    rows = jnp.where(slot_here(count_s[...], piece), hot_s[...], 0.0)
    send[...] = jnp.dot(spread(rows), tok_s[...], preferred_element_type=F32).astype(BF)


def scale_kernel(ids, place, gates, cot, send, turned, hot_s, count_s, gate_s, cot_s):
    piece = pl.program_id(0)

    @pl.when(piece == 0)
    def _():
        hot, count = routing(ids, place)
        hot_s[...] = eightfold(hot[0] + hot[1])
        count_s[...] = eightfold(count)
        gate_s[...] = eightfold(hot[0] * gates[0:1, :] + hot[1] * gates[1:2, :])
        cot_s[...] = stacked(cot)

    here = slot_here(count_s[...], piece)
    rows = jnp.where(here, gate_s[...], 0.0)
    send[...] = jnp.dot(spread(rows), cot_s[...], preferred_element_type=F32).astype(BF)
    turned[...] = spread_turned(jnp.where(here, hot_s[...], 0.0).T)


def combine_kernel(turned, back, out):
    total = sum(
        jnp.dot(
            turned[p * PACKED : (p + 1) * PACKED, :],
            back[:, p * WIDE : (p + 1) * WIDE],
            preferred_element_type=F32,
        )
        for p in range(PIECES)
    ).astype(BF)
    for c in range(SHARDS):
        out[:, c * WIDE : (c + 1) * WIDE] = total[c * TOK : (c + 1) * TOK, :]


def packing(member, turned):
    shape = (256, 256)
    outer, inner = iota(shape, 1 if turned else 0), iota(shape, 0 if turned else 1)
    within = outer % 64
    chunk = (member + outer // 64) % SHARDS
    return (inner == (within // 2) * 8 + chunk * 2 + within % 2).astype(BF)


def unpack(packed, order, blocks, piece):
    for half in range(2):
        block = jnp.dot(
            order,
            packed[half * 256 : half * 256 + 256, piece * WIDE : (piece + 1) * WIDE],
            preferred_element_type=F32,
        ).astype(BF)
        start = (piece * 2 + half) * 64
        for k in range(SHARDS):
            blocks[k][start : start + 64, :] = block[k * 64 : k * 64 + 64, :]


def copies_of(parts, dest, sems, base):
    own, right, opp_a, opp_b, left = parts
    half = opp_a.shape[0]
    pairs = (
        (own, dest.at[0]),
        (right, dest.at[1]),
        (opp_a, dest.at[2, pl.ds(0, half)]),
        (opp_b, dest.at[2, pl.ds(half, half)]),
        (left, dest.at[3]),
    )
    return [pltpu.make_async_copy(s, d, sems.at[base + n]) for n, (s, d) in enumerate(pairs)]


def begin(copies):
    for copy in copies:
        copy.start()


def finish(copies):
    for copy in copies:
        copy.wait()


def unpack_kernel(info, recv, *blocks):
    order = packing(info[0], False)
    for piece in range(PIECES):
        unpack(recv, order, blocks, piece)


def forward_kernel(info, *refs):
    blocks = refs[0:4]
    gate_parts, up_parts = refs[4:9], refs[9:14]
    hidden, slope_gate, slope_up = refs[14:17]
    gate_v, up_v, sems = refs[17:]
    copies = copies_of(gate_parts, gate_v, sems, 0) + copies_of(up_parts, up_v, sems, 5)
    begin(copies)
    finish(copies)
    pre_gate = jnp.zeros((ROWS, HID), F32)
    pre_up = jnp.zeros((ROWS, HID), F32)
    for k in range(SHARDS):
        x = blocks[k][...]
        pre_gate += jnp.dot(x, gate_v[k], preferred_element_type=F32)
        pre_up += jnp.dot(x, up_v[k], preferred_element_type=F32)
    sigma = jax.nn.sigmoid(pre_gate)
    silu = pre_gate * sigma
    live = iota((ROWS, HID), 1) < info[1]
    hidden[...] = jnp.where(live, silu * pre_up, 0.0).astype(BF)
    slope_gate[...] = jnp.where(live, pre_up * sigma * (1.0 + pre_gate * (1.0 - sigma)), 0.0)
    slope_up[...] = jnp.where(live, silu, 0.0)


def dot_turned(x, w):
    return lax.dot_general(x, w, (((1,), (1,)), ((), ())), preferred_element_type=F32)


def backward_kernel(info, recv, slope_gate, slope_up, *refs):
    down_parts, gate_parts, up_parts = refs[0:5], refs[5:10], refs[10:15]
    rows_out = refs[15:19]
    d_out, send = refs[19:21]
    recv_v, slope_gate_v, slope_up_v, down_v, gate_v, up_v = refs[21:27]
    blocks = refs[27:31]
    held, send_v, sems = refs[31:]
    columns = [pl.ds(piece * WIDE, WIDE) for piece in range(PIECES)]
    loads = [
        pltpu.make_async_copy(recv.at[:, columns[n]], recv_v.at[:, columns[n]], sems.at[25 + n])
        for n in range(PIECES)
    ]
    down = copies_of(down_parts, down_v, sems, 3)
    slopes = [
        pltpu.make_async_copy(slope_gate, slope_gate_v, sems.at[1]),
        pltpu.make_async_copy(slope_up, slope_up_v, sems.at[2]),
    ]
    gate = copies_of(gate_parts, gate_v, sems, 8)
    up = copies_of(up_parts, up_v, sems, 13)
    begin(loads)
    order = packing(info[0], False)
    loads[0].wait()
    begin(down[:2])
    unpack(recv_v, order, blocks, 0)
    loads[1].wait()
    begin(down[2:])
    unpack(recv_v, order, blocks, 1)
    loads[2].wait()
    begin(slopes)
    unpack(recv_v, order, blocks, 2)
    shards = ((0,), (1,), (2, 3), (4,))
    grad = jnp.zeros((ROWS, HID), F32)
    for k in range(SHARDS):
        for n in shards[k]:
            down[n].wait()
            gate[n].start()
            up[n].start()
        grad += dot_turned(blocks[k][...], down_v[k])
    finish(slopes)
    outs = [
        pltpu.make_async_copy(blocks[k], rows_out[k], sems.at[18 + k]) for k in range(SHARDS)
    ]
    d_gate = (grad * slope_gate_v[...]).astype(BF)
    d_up = (grad * slope_up_v[...]).astype(BF)
    d_out[:, :HID] = d_gate
    d_out[:, HID:] = d_up
    for k in range(SHARDS):
        for n in shards[k]:
            gate[n].wait()
            up[n].wait()
        outs[k].start()
        part = (
            dot_turned(d_out[:, :HID], gate_v[k]) + dot_turned(d_out[:, HID:], up_v[k])
        ).astype(BF)
        for n in range(2 * PIECES):
            held[n * 256 + k * 64 : n * 256 + k * 64 + 64, :] = part[n * 64 : n * 64 + 64, :]
    back = packing(info[0], True)
    for piece in range(PIECES):
        for half in range(2):
            start = (piece * 2 + half) * 256
            send_v[piece, half * 256 : half * 256 + 256, :] = jnp.dot(
                back, held[start : start + 256, :], preferred_element_type=F32
            ).astype(BF)
        copy = pltpu.make_async_copy(
            send_v.at[piece], send.at[:, columns[piece]], sems.at[22 + piece]
        )
        copy.start()
        outs.append(copy)
    finish(outs)


def halves_kernel(left, right, top, bottom, sems):
    half = top.shape[0]
    copies = [
        pltpu.make_async_copy(left.at[pl.ds(0, half)], top, sems.at[0]),
        pltpu.make_async_copy(right.at[pl.ds(half, half)], bottom, sems.at[1]),
    ]
    begin(copies)
    finish(copies)


RIGHT = [(n, (n + 1) % SHARDS) for n in range(SHARDS)]
LEFT = [(n, (n - 1) % SHARDS) for n in range(SHARDS)]


def to_right(x):
    return lax.ppermute(x, "dp", RIGHT)


def to_left(x):
    return lax.ppermute(x, "dp", LEFT)


def near(own):
    return to_right(own), to_left(own)


def far(left, right):
    half = left.shape[0] // 2
    return to_right(left[:half]), to_left(right[half:])


def scatter(own, right, opp, left):
    half = opp.shape[0] // 2
    narrow = lambda v: v.astype(BF)
    wide = lambda v: v.astype(F32)
    from_left = to_right(narrow(opp[:half]))
    from_right = to_left(narrow(opp[half:]))
    left_b = to_right(narrow(right[half:]))
    right_a = to_left(narrow(left[:half]))
    left_a = to_right(narrow(right[:half] + wide(from_left)))
    right_b = to_left(narrow(left[half:] + wide(from_right)))
    top = narrow(own[:half] + wide(left_a) + wide(right_a))
    bottom = narrow(own[half:] + wide(left_b) + wide(right_b))
    return jnp.concatenate([top, bottom], axis=0)


def exchange(x):
    return lax.all_to_all(
        x.reshape(CORES, 8, PIECES * WIDE), "expert", split_axis=0, concat_axis=0, tiled=True
    ).reshape(PACKED, PIECES * WIDE)


PACKED_TYPE = jax.ShapeDtypeStruct((PACKED, PIECES * WIDE), BF)
BLOCK_TYPE = jax.ShapeDtypeStruct((ROWS, WIDE), BF)
HID_BF = jax.ShapeDtypeStruct((ROWS, HID), BF)
HID_F32 = jax.ShapeDtypeStruct((ROWS, HID), F32)
WEIGHT = pltpu.VMEM((SHARDS, WIDE, HID), BF)
PACKED_V = pltpu.VMEM((PACKED, PIECES * WIDE), BF)
MAPPED = pltpu.VMEM((PACKED, TOK), F32)
TALL = pltpu.VMEM((PACKED, WIDE), BF)
TURNED_ROWS = pl.BlockSpec((PACKED, PACKED), lambda p: (p, 0))
PIECE_COLS = pl.BlockSpec((PACKED, WIDE), lambda p: (0, p))


def whole(*shape):
    return pl.BlockSpec(shape, lambda p: (0, 0))


def call(kernel, flops, nbytes, mib, name, **rest):
    return pl.pallas_call(
        kernel,
        compiler_params=pltpu.CompilerParams(vmem_limit_bytes=mib * MIB),
        cost_estimate=pl.CostEstimate(flops=flops, bytes_accessed=nbytes, transcendentals=0),
        name=name,
        **rest,
    )


def run_route(ids, place, tokens):
    return call(
        route_kernel, 1_700_000_000, 5_000_000, 62, "route",
        grid=(PIECES,),
        in_specs=[whole(2, TOK), whole(1, CORES), whole(TOK, SHARDS * WIDE)],
        out_specs=PIECE_COLS,
        out_shape=PACKED_TYPE,
        scratch_shapes=[MAPPED, MAPPED, TALL],
    )(ids, place, tokens)


def run_scale(ids, place, gates, cotangent):
    return call(
        scale_kernel, 1_700_000_000, 6_000_000, 62, "scale",
        grid=(PIECES,),
        in_specs=[whole(2, TOK), whole(1, CORES), whole(2, TOK), whole(TOK, SHARDS * WIDE)],
        out_specs=[PIECE_COLS, TURNED_ROWS],
        out_shape=[PACKED_TYPE, jax.ShapeDtypeStruct((PIECES * PACKED, PACKED), BF)],
        scratch_shapes=[MAPPED, MAPPED, MAPPED, TALL],
    )(ids, place, gates, cotangent)


def run_unpack(info, recv):
    return call(
        unpack_kernel, 800_000_000, 6_000_000, 62, "unpack",
        in_specs=[SMEM, VMEM],
        out_specs=[VMEM] * 4,
        out_shape=[BLOCK_TYPE] * 4,
    )(info, recv)


def run_forward(info, blocks, gate_parts, up_parts):
    return call(
        forward_kernel, 3_300_000_000, 14_000_000, 62, "forward",
        in_specs=[SMEM] + [VMEM] * 4 + [ANY] * 10,
        out_specs=[VMEM] * 3,
        out_shape=[HID_BF, HID_F32, HID_F32],
        scratch_shapes=[WEIGHT, WEIGHT, pltpu.SemaphoreType.DMA((10,))],
    )(info, *blocks, *gate_parts, *up_parts)


def run_backward(info, recv, slope_gate, slope_up, down_parts, gate_parts, up_parts):
    return call(
        backward_kernel, 7_000_000_000, 26_000_000, 62, "backward",
        in_specs=[SMEM] + [ANY] * 18,
        out_specs=[ANY] * 4 + [VMEM, ANY],
        out_shape=[BLOCK_TYPE] * 4 + [BLOCK_TYPE, PACKED_TYPE],
        scratch_shapes=[
            PACKED_V,
            pltpu.VMEM((ROWS, HID), F32),
            pltpu.VMEM((ROWS, HID), F32),
            pltpu.VMEM((SHARDS, HID, WIDE), BF),
            WEIGHT,
            WEIGHT,
            *[pltpu.VMEM((ROWS, WIDE), BF)] * 4,
            pltpu.VMEM((2 * PIECES * 256, WIDE), BF),
            pltpu.VMEM((PIECES, PACKED, WIDE), BF),
            pltpu.SemaphoreType.DMA((28,)),
        ],
    )(info, recv, slope_gate, slope_up, *down_parts, *gate_parts, *up_parts)


def run_combine(turned, recv):
    return call(
        combine_kernel, 1_700_000_000, 5_000_000, 16, "combine",
        in_specs=[VMEM] * 2,
        out_specs=VMEM,
        out_shape=jax.ShapeDtypeStruct((TOK, SHARDS * WIDE), BF),
    )(turned, recv)


def run_halves(left, right, flops):
    half = jax.ShapeDtypeStruct((left.shape[0] // 2, left.shape[1]), BF)
    return call(
        halves_kernel, flops, 2_000_000, 62, "halves",
        in_specs=[ANY] * 2,
        out_specs=[ANY] * 2,
        out_shape=[half] * 2,
        scratch_shapes=[pltpu.SemaphoreType.DMA((2,))],
    )(left, right)


def on_device(tokens, cotangent, expert_ids, gates, widths, placement, w_gate, w_up, w_down):
    experts = jnp.arange(CORES, dtype=jnp.int32)
    owner = jnp.sum(jnp.where(placement == lax.axis_index("expert"), experts, 0))
    width = jnp.sum(jnp.where(experts == owner, widths, 0))
    info = jnp.stack([lax.axis_index("dp").astype(jnp.int32), width])
    shards = (w_gate[0], w_up[0], w_down[0])
    nears = [near(w) for w in shards]
    ids = expert_ids.T
    place = placement[None]

    recv_x = exchange(run_route(ids, place, tokens))
    send_g, turned = run_scale(ids, place, gates.astype(F32).T, cotangent)
    send_g, nears, info = lax.optimization_barrier((send_g, nears, info))
    recv_g = exchange(send_g)
    parts = []
    for own, (left, right) in zip(shards, nears):
        opp_a, opp_b = far(left, right)
        parts.append((own, right, opp_a, opp_b, left))
    gate_parts, up_parts, down_parts = parts

    blocks_x = run_unpack(info, recv_x)
    mid = ROWS // 2
    x_left, x_right = to_right(blocks_x[1]), to_left(blocks_x[3])
    x_passing = to_right(blocks_x[2][:mid]), to_left(blocks_x[2][mid:])

    hidden, slope_gate, slope_up = run_forward(info, blocks_x, gate_parts, up_parts)
    recv_g, x_left, x_right, x_passing = lax.optimization_barrier(
        (recv_g, x_left, x_right, x_passing)
    )
    x_far = to_right(x_passing[0]), to_left(x_passing[1])

    *blocks_g, d, send_d = run_backward(
        info, recv_g, slope_gate, slope_up, down_parts, gate_parts, up_parts
    )
    recv_d = exchange(send_d)

    dot = functools.partial(jnp.einsum, "ra,rb->ab", preferred_element_type=F32)
    left, right = near(d)
    top, bottom = run_halves(left, right, 100_000_000_000)
    opp_a, opp_b = to_right(top), to_left(bottom)
    pairs = (
        (blocks_x[0], d), (x_left, left), (x_right, right), (x_far[0], opp_a), (x_far[1], opp_b)
    )
    grads = sum(dot(x, y) for x, y in pairs).astype(BF)
    grad_gate, grad_up = grads[:, :HID], grads[:, HID:]
    grad_down = scatter(*[dot(hidden, block) for block in blocks_g])
    grad_tokens = run_combine(turned, recv_d)
    return (grad_tokens, grad_gate[None], grad_up[None], grad_down[None])


def solution(mesh):
    placed = (
        P(("dp", "expert"), None),
        P(("dp", "expert"), None),
        P(("dp", "expert"), None),
        P(("dp", "expert"), None),
        P(),
        P(),
        P("expert", "dp", None),
        P("expert", "dp", None),
        P("expert", None, "dp"),
    )
    return jax.shard_map(
        on_device,
        mesh=mesh,
        in_specs=placed,
        out_specs=(
            P(("dp", "expert"), None),
            P("expert", "dp", None),
            P("expert", "dp", None),
            P("expert", None, "dp"),
        ),
        check_vma=False,
    )
```

```python
import functools

import jax
import jax.numpy as jnp
from jax import lax
from jax.experimental import pallas as pl
from jax.experimental.pallas import tpu as pltpu
from jax.sharding import PartitionSpec as P

BF = jnp.bfloat16
F32 = jnp.float32
SHARDS = 4
SLOTS = 6
PIECES = 3
CORES = 64
TOK = 128
WIDE = 1024
HID = 512
ROWS = CORES * SLOTS
PACKED = CORES * 8
VMEM = pl.BlockSpec(memory_space=pltpu.VMEM)
SMEM = pl.BlockSpec(memory_space=pltpu.SMEM)
ANY = pl.BlockSpec(memory_space=pl.ANY)
MIB = 1024 * 1024


def iota(shape, dim):
    return lax.broadcasted_iota(jnp.int32, shape, dim)


def spread(rows):
    chunk = (iota((PACKED, TOK), 0) % 8) // 2
    return jnp.concatenate(
        [jnp.where(chunk == c, rows, 0.0).astype(BF) for c in range(SHARDS)], axis=1
    )


def spread_turned(rows):
    chunk = (iota((TOK, PACKED), 1) % 8) // 2
    return jnp.concatenate(
        [jnp.where(chunk == c, rows, 0.0).astype(BF) for c in range(SHARDS)], axis=0
    )


def stacked(ref):
    return jnp.concatenate([ref[:, c * WIDE : (c + 1) * WIDE] for c in range(SHARDS)], axis=0)


def routing(ids, place):
    expert = iota((CORES, TOK), 0)
    slot_of = (iota((CORES, CORES), 0) == place[0:1, :]).astype(BF)
    hot = [
        jnp.dot(slot_of, (ids[k : k + 1, :] == expert).astype(BF), preferred_element_type=F32)
        for k in range(2)
    ]
    before = (iota((TOK, TOK), 0) < iota((TOK, TOK), 1)).astype(BF)
    count = jnp.dot((hot[0] + hot[1]).astype(BF), before, preferred_element_type=F32)
    return hot, count


def eightfold(x):
    return jnp.broadcast_to(x[:, None, :], (CORES, 8, TOK)).reshape(PACKED, TOK)


def slot_here(count, piece):
    return count == (2 * piece + iota((PACKED, TOK), 0) % 2).astype(F32)


def route_kernel(ids, place, tok, send, hot_s, count_s, tok_s):
    piece = pl.program_id(0)

    @pl.when(piece == 0)
    def _():
        hot, count = routing(ids, place)
        hot_s[...] = eightfold(hot[0] + hot[1])
        count_s[...] = eightfold(count)
        tok_s[...] = stacked(tok)

    rows = jnp.where(slot_here(count_s[...], piece), hot_s[...], 0.0)
    send[...] = jnp.dot(spread(rows), tok_s[...], preferred_element_type=F32).astype(BF)


def scale_kernel(ids, place, gates, cot, send, turned, hot_s, count_s, gate_s, cot_s):
    piece = pl.program_id(0)

    @pl.when(piece == 0)
    def _():
        hot, count = routing(ids, place)
        hot_s[...] = eightfold(hot[0] + hot[1])
        count_s[...] = eightfold(count)
        gate_s[...] = eightfold(hot[0] * gates[0:1, :] + hot[1] * gates[1:2, :])
        cot_s[...] = stacked(cot)

    here = slot_here(count_s[...], piece)
    rows = jnp.where(here, gate_s[...], 0.0)
    send[...] = jnp.dot(spread(rows), cot_s[...], preferred_element_type=F32).astype(BF)
    turned[...] = spread_turned(jnp.where(here, hot_s[...], 0.0).T)


def combine_kernel(turned, back, out):
    total = sum(
        jnp.dot(
            turned[p * PACKED : (p + 1) * PACKED, :],
            back[:, p * WIDE : (p + 1) * WIDE],
            preferred_element_type=F32,
        )
        for p in range(PIECES)
    ).astype(BF)
    for c in range(SHARDS):
        out[:, c * WIDE : (c + 1) * WIDE] = total[c * TOK : (c + 1) * TOK, :]


def packing(member, turned):
    shape = (256, 256)
    outer, inner = iota(shape, 1 if turned else 0), iota(shape, 0 if turned else 1)
    within = outer % 64
    chunk = (member + outer // 64) % SHARDS
    return (inner == (within // 2) * 8 + chunk * 2 + within % 2).astype(BF)


def unpack(packed, order, blocks, piece):
    for half in range(2):
        block = jnp.dot(
            order,
            packed[half * 256 : half * 256 + 256, piece * WIDE : (piece + 1) * WIDE],
            preferred_element_type=F32,
        ).astype(BF)
        start = (piece * 2 + half) * 64
        for k in range(SHARDS):
            blocks[k][start : start + 64, :] = block[k * 64 : k * 64 + 64, :]


def copies_of(parts, dest, sems, base):
    own, right, opp_a, opp_b, left = parts
    half = opp_a.shape[0]
    pairs = (
        (own, dest.at[0]),
        (right, dest.at[1]),
        (opp_a, dest.at[2, pl.ds(0, half)]),
        (opp_b, dest.at[2, pl.ds(half, half)]),
        (left, dest.at[3]),
    )
    return [pltpu.make_async_copy(s, d, sems.at[base + n]) for n, (s, d) in enumerate(pairs)]


def begin(copies):
    for copy in copies:
        copy.start()


def finish(copies):
    for copy in copies:
        copy.wait()


def unpack_kernel(info, recv, *blocks):
    order = packing(info[0], False)
    for piece in range(PIECES):
        unpack(recv, order, blocks, piece)


def forward_kernel(info, *refs):
    blocks = refs[0:4]
    gate_parts, up_parts = refs[4:9], refs[9:14]
    hidden, slope_gate, slope_up = refs[14:17]
    gate_v, up_v, sems = refs[17:]
    copies = copies_of(gate_parts, gate_v, sems, 0) + copies_of(up_parts, up_v, sems, 5)
    begin(copies)
    finish(copies)
    pre_gate = jnp.zeros((ROWS, HID), F32)
    pre_up = jnp.zeros((ROWS, HID), F32)
    for k in range(SHARDS):
        x = blocks[k][...]
        pre_gate += jnp.dot(x, gate_v[k], preferred_element_type=F32)
        pre_up += jnp.dot(x, up_v[k], preferred_element_type=F32)
    sigma = jax.nn.sigmoid(pre_gate)
    silu = pre_gate * sigma
    live = iota((ROWS, HID), 1) < info[1]
    hidden[...] = jnp.where(live, silu * pre_up, 0.0).astype(BF)
    slope_gate[...] = jnp.where(live, pre_up * sigma * (1.0 + pre_gate * (1.0 - sigma)), 0.0)
    slope_up[...] = jnp.where(live, silu, 0.0)


def dot_turned(x, w):
    return lax.dot_general(x, w, (((1,), (1,)), ((), ())), preferred_element_type=F32)


def backward_kernel(info, recv, slope_gate, slope_up, *refs):
    down_parts, gate_parts, up_parts = refs[0:5], refs[5:10], refs[10:15]
    rows_out = refs[15:19]
    d_out, send = refs[19:21]
    recv_v, slope_gate_v, slope_up_v, down_v, gate_v, up_v = refs[21:27]
    blocks = refs[27:31]
    held, send_v, sems = refs[31:]
    columns = [pl.ds(piece * WIDE, WIDE) for piece in range(PIECES)]
    loads = [
        pltpu.make_async_copy(recv.at[:, columns[n]], recv_v.at[:, columns[n]], sems.at[25 + n])
        for n in range(PIECES)
    ]
    down = copies_of(down_parts, down_v, sems, 3)
    slopes = [
        pltpu.make_async_copy(slope_gate, slope_gate_v, sems.at[1]),
        pltpu.make_async_copy(slope_up, slope_up_v, sems.at[2]),
    ]
    gate = copies_of(gate_parts, gate_v, sems, 8)
    up = copies_of(up_parts, up_v, sems, 13)
    begin(loads)
    order = packing(info[0], False)
    loads[0].wait()
    begin(down[:2])
    unpack(recv_v, order, blocks, 0)
    loads[1].wait()
    begin(down[2:])
    unpack(recv_v, order, blocks, 1)
    loads[2].wait()
    begin(slopes)
    unpack(recv_v, order, blocks, 2)
    shards = ((0,), (1,), (2, 3), (4,))
    grad = jnp.zeros((ROWS, HID), F32)
    for k in range(SHARDS):
        for n in shards[k]:
            down[n].wait()
            gate[n].start()
            up[n].start()
        grad += dot_turned(blocks[k][...], down_v[k])
    finish(slopes)
    outs = [
        pltpu.make_async_copy(blocks[k], rows_out[k], sems.at[18 + k]) for k in range(SHARDS)
    ]
    d_gate = (grad * slope_gate_v[...]).astype(BF)
    d_up = (grad * slope_up_v[...]).astype(BF)
    d_out[:, :HID] = d_gate
    d_out[:, HID:] = d_up
    for k in range(SHARDS):
        for n in shards[k]:
            gate[n].wait()
            up[n].wait()
        outs[k].start()
        part = (
            dot_turned(d_out[:, :HID], gate_v[k]) + dot_turned(d_out[:, HID:], up_v[k])
        ).astype(BF)
        for n in range(2 * PIECES):
            held[n * 256 + k * 64 : n * 256 + k * 64 + 64, :] = part[n * 64 : n * 64 + 64, :]
    back = packing(info[0], True)
    for piece in range(PIECES):
        for half in range(2):
            start = (piece * 2 + half) * 256
            send_v[piece, half * 256 : half * 256 + 256, :] = jnp.dot(
                back, held[start : start + 256, :], preferred_element_type=F32
            ).astype(BF)
        copy = pltpu.make_async_copy(
            send_v.at[piece], send.at[:, columns[piece]], sems.at[22 + piece]
        )
        copy.start()
        outs.append(copy)
    finish(outs)


def halves_kernel(left, right, top, bottom):
    half = top.shape[0]
    top[...] = left[:half, :]
    bottom[...] = right[right.shape[0] - half :, :]


RIGHT = [(n, (n + 1) % SHARDS) for n in range(SHARDS)]
LEFT = [(n, (n - 1) % SHARDS) for n in range(SHARDS)]


def to_right(x):
    return lax.ppermute(x, "dp", RIGHT)


def to_left(x):
    return lax.ppermute(x, "dp", LEFT)


def near(own):
    return to_right(own), to_left(own)


def far(left, right):
    half = left.shape[0] // 2
    return to_right(left[:half]), to_left(right[half:])


def scatter(own, right, opp, left):
    half = opp.shape[0] // 2
    narrow = lambda v: v.astype(BF)
    wide = lambda v: v.astype(F32)
    from_left = to_right(narrow(opp[:half]))
    from_right = to_left(narrow(opp[half:]))
    left_b = to_right(narrow(right[half:]))
    right_a = to_left(narrow(left[:half]))
    left_a = to_right(narrow(right[:half] + wide(from_left)))
    right_b = to_left(narrow(left[half:] + wide(from_right)))
    top = narrow(own[:half] + wide(left_a) + wide(right_a))
    bottom = narrow(own[half:] + wide(left_b) + wide(right_b))
    return jnp.concatenate([top, bottom], axis=0)


def exchange(x):
    return lax.all_to_all(
        x.reshape(CORES, 8, PIECES * WIDE), "expert", split_axis=0, concat_axis=0, tiled=True
    ).reshape(PACKED, PIECES * WIDE)


PACKED_TYPE = jax.ShapeDtypeStruct((PACKED, PIECES * WIDE), BF)
BLOCK_TYPE = jax.ShapeDtypeStruct((ROWS, WIDE), BF)
HID_BF = jax.ShapeDtypeStruct((ROWS, HID), BF)
HID_F32 = jax.ShapeDtypeStruct((ROWS, HID), F32)
WEIGHT = pltpu.VMEM((SHARDS, WIDE, HID), BF)
PACKED_V = pltpu.VMEM((PACKED, PIECES * WIDE), BF)
MAPPED = pltpu.VMEM((PACKED, TOK), F32)
TALL = pltpu.VMEM((PACKED, WIDE), BF)
TURNED_ROWS = pl.BlockSpec((PACKED, PACKED), lambda p: (p, 0))
PIECE_COLS = pl.BlockSpec((PACKED, WIDE), lambda p: (0, p))


def whole(*shape):
    return pl.BlockSpec(shape, lambda p: (0, 0))


def call(kernel, flops, nbytes, mib, name, **rest):
    return pl.pallas_call(
        kernel,
        compiler_params=pltpu.CompilerParams(vmem_limit_bytes=mib * MIB),
        cost_estimate=pl.CostEstimate(flops=flops, bytes_accessed=nbytes, transcendentals=0),
        name=name,
        **rest,
    )


def run_route(ids, place, tokens):
    return call(
        route_kernel, 1_700_000_000, 5_000_000, 62, "route",
        grid=(PIECES,),
        in_specs=[whole(2, TOK), whole(1, CORES), whole(TOK, SHARDS * WIDE)],
        out_specs=PIECE_COLS,
        out_shape=PACKED_TYPE,
        scratch_shapes=[MAPPED, MAPPED, TALL],
    )(ids, place, tokens)


def run_scale(ids, place, gates, cotangent):
    return call(
        scale_kernel, 1_700_000_000, 6_000_000, 62, "scale",
        grid=(PIECES,),
        in_specs=[whole(2, TOK), whole(1, CORES), whole(2, TOK), whole(TOK, SHARDS * WIDE)],
        out_specs=[PIECE_COLS, TURNED_ROWS],
        out_shape=[PACKED_TYPE, jax.ShapeDtypeStruct((PIECES * PACKED, PACKED), BF)],
        scratch_shapes=[MAPPED, MAPPED, MAPPED, TALL],
    )(ids, place, gates, cotangent)


def run_unpack(info, recv):
    return call(
        unpack_kernel, 800_000_000, 6_000_000, 62, "unpack",
        in_specs=[SMEM, VMEM],
        out_specs=[VMEM] * 4,
        out_shape=[BLOCK_TYPE] * 4,
    )(info, recv)


def run_forward(info, blocks, gate_parts, up_parts):
    return call(
        forward_kernel, 3_300_000_000, 14_000_000, 62, "forward",
        in_specs=[SMEM] + [VMEM] * 4 + [ANY] * 10,
        out_specs=[VMEM] * 3,
        out_shape=[HID_BF, HID_F32, HID_F32],
        scratch_shapes=[WEIGHT, WEIGHT, pltpu.SemaphoreType.DMA((10,))],
    )(info, *blocks, *gate_parts, *up_parts)


def run_backward(info, recv, slope_gate, slope_up, down_parts, gate_parts, up_parts):
    return call(
        backward_kernel, 7_000_000_000, 26_000_000, 62, "backward",
        in_specs=[SMEM] + [ANY] * 18,
        out_specs=[ANY] * 4 + [VMEM, ANY],
        out_shape=[BLOCK_TYPE] * 4 + [BLOCK_TYPE, PACKED_TYPE],
        scratch_shapes=[
            PACKED_V,
            pltpu.VMEM((ROWS, HID), F32),
            pltpu.VMEM((ROWS, HID), F32),
            pltpu.VMEM((SHARDS, HID, WIDE), BF),
            WEIGHT,
            WEIGHT,
            *[pltpu.VMEM((ROWS, WIDE), BF)] * 4,
            pltpu.VMEM((2 * PIECES * 256, WIDE), BF),
            pltpu.VMEM((PIECES, PACKED, WIDE), BF),
            pltpu.SemaphoreType.DMA((28,)),
        ],
    )(info, recv, slope_gate, slope_up, *down_parts, *gate_parts, *up_parts)


def run_combine(turned, recv):
    return call(
        combine_kernel, 1_700_000_000, 5_000_000, 16, "combine",
        in_specs=[VMEM] * 2,
        out_specs=VMEM,
        out_shape=jax.ShapeDtypeStruct((TOK, SHARDS * WIDE), BF),
    )(turned, recv)


def run_halves(left, right, rows, flops):
    half = jax.ShapeDtypeStruct((rows, left.shape[1]), BF)
    return call(
        halves_kernel, flops, 2_000_000, 62, "halves",
        in_specs=[VMEM] * 2,
        out_specs=[VMEM] * 2,
        out_shape=[half] * 2,
    )(left, right)


def on_device(tokens, cotangent, expert_ids, gates, widths, placement, w_gate, w_up, w_down):
    experts = jnp.arange(CORES, dtype=jnp.int32)
    owner = jnp.sum(jnp.where(placement == lax.axis_index("expert"), experts, 0))
    width = jnp.sum(jnp.where(experts == owner, widths, 0))
    info = jnp.stack([lax.axis_index("dp").astype(jnp.int32), width])
    shards = (w_gate[0], w_up[0], w_down[0])
    nears = [near(w) for w in shards]
    ids = expert_ids.T
    place = placement[None]

    recv_x = exchange(run_route(ids, place, tokens))
    send_g, turned = run_scale(ids, place, gates.astype(F32).T, cotangent)
    mid = WIDE // 2
    top, bottom = run_halves(*nears[0], mid, 1_000_000)
    gate_far = run_halves(to_right(top), to_left(bottom), mid, 70_000_000_000)
    send_g, info, nears[0], nears[1] = lax.optimization_barrier(
        (send_g, info, nears[0], nears[1])
    )
    recv_g = exchange(send_g)
    top, bottom = run_halves(*nears[2], HID // 2, 30_000_000_000)
    fars = gate_far, far(*nears[1]), (to_right(top), to_left(bottom))
    gate_parts, up_parts, down_parts = [
        (own, right, opp_a, opp_b, left)
        for own, (left, right), (opp_a, opp_b) in zip(shards, nears, fars)
    ]

    info, gate_parts = lax.optimization_barrier((info, gate_parts))
    blocks_x = run_unpack(info, recv_x)
    mid = ROWS // 2
    x_left, x_right = to_right(blocks_x[1]), to_left(blocks_x[3])
    x_passing = to_right(blocks_x[2][:mid]), to_left(blocks_x[2][mid:])

    hidden, slope_gate, slope_up = run_forward(info, blocks_x, gate_parts, up_parts)
    x_far = to_right(x_passing[0]), to_left(x_passing[1])
    recv_g, x_left, x_right, x_far = lax.optimization_barrier((recv_g, x_left, x_right, x_far))

    *blocks_g, d, send_d = run_backward(
        info, recv_g, slope_gate, slope_up, down_parts, gate_parts, up_parts
    )
    recv_d = exchange(send_d)

    dot = functools.partial(jnp.einsum, "ra,rb->ab", preferred_element_type=F32)
    left, right = near(d)
    opp_a, opp_b = far(left, right)
    pairs = (
        (blocks_x[0], d), (x_left, left), (x_right, right), (x_far[0], opp_a), (x_far[1], opp_b)
    )
    grads = sum(dot(x, y) for x, y in pairs).astype(BF)
    grad_gate, grad_up = grads[:, :HID], grads[:, HID:]
    grad_down = scatter(*[dot(hidden, block) for block in blocks_g])
    grad_tokens = run_combine(turned, recv_d)
    return (grad_tokens, grad_gate[None], grad_up[None], grad_down[None])


def solution(mesh):
    placed = (
        P(("dp", "expert"), None),
        P(("dp", "expert"), None),
        P(("dp", "expert"), None),
        P(("dp", "expert"), None),
        P(),
        P(),
        P("expert", "dp", None),
        P("expert", "dp", None),
        P("expert", None, "dp"),
    )
    return jax.shard_map(
        on_device,
        mesh=mesh,
        in_specs=placed,
        out_specs=(
            P(("dp", "expert"), None),
            P("expert", "dp", None),
            P("expert", "dp", None),
            P("expert", None, "dp"),
        ),
        check_vma=False,
    )
```

```python
import functools

import jax
import jax.numpy as jnp
from jax import lax
from jax.experimental import pallas as pl
from jax.experimental.pallas import tpu as pltpu
from jax.sharding import PartitionSpec as P

BF = jnp.bfloat16
F32 = jnp.float32
SHARDS = 4
SLOTS = 6
PIECES = 3
CORES = 64
TOK = 128
WIDE = 1024
HID = 512
ROWS = CORES * SLOTS
PACKED = CORES * 8
VMEM = pl.BlockSpec(memory_space=pltpu.VMEM)
SMEM = pl.BlockSpec(memory_space=pltpu.SMEM)
ANY = pl.BlockSpec(memory_space=pl.ANY)
MIB = 1024 * 1024


def iota(shape, dim):
    return lax.broadcasted_iota(jnp.int32, shape, dim)


def spread(rows):
    chunk = (iota((PACKED, TOK), 0) % 8) // 2
    return jnp.concatenate(
        [jnp.where(chunk == c, rows, 0.0).astype(BF) for c in range(SHARDS)], axis=1
    )


def spread_turned(rows):
    chunk = (iota((TOK, PACKED), 1) % 8) // 2
    return jnp.concatenate(
        [jnp.where(chunk == c, rows, 0.0).astype(BF) for c in range(SHARDS)], axis=0
    )


def stacked(ref):
    return jnp.concatenate([ref[:, c * WIDE : (c + 1) * WIDE] for c in range(SHARDS)], axis=0)


def routing(ids, place):
    expert = iota((CORES, TOK), 0)
    slot_of = (iota((CORES, CORES), 0) == place[0:1, :]).astype(BF)
    hot = [
        jnp.dot(slot_of, (ids[k : k + 1, :] == expert).astype(BF), preferred_element_type=F32)
        for k in range(2)
    ]
    before = (iota((TOK, TOK), 0) < iota((TOK, TOK), 1)).astype(BF)
    count = jnp.dot((hot[0] + hot[1]).astype(BF), before, preferred_element_type=F32)
    return hot, count


def eightfold(x):
    return jnp.broadcast_to(x[:, None, :], (CORES, 8, TOK)).reshape(PACKED, TOK)


def slot_here(count, piece):
    return count == (2 * piece + iota((PACKED, TOK), 0) % 2).astype(F32)


def route_kernel(ids, place, tok, send, hot_s, count_s, tok_s):
    piece = pl.program_id(0)

    @pl.when(piece == 0)
    def _():
        hot, count = routing(ids, place)
        hot_s[...] = eightfold(hot[0] + hot[1])
        count_s[...] = eightfold(count)
        tok_s[...] = stacked(tok)

    rows = jnp.where(slot_here(count_s[...], piece), hot_s[...], 0.0)
    send[...] = jnp.dot(spread(rows), tok_s[...], preferred_element_type=F32).astype(BF)


def scale_kernel(ids, place, gates, cot, send, turned, hot_s, count_s, gate_s, cot_s):
    piece = pl.program_id(0)

    @pl.when(piece == 0)
    def _():
        hot, count = routing(ids, place)
        hot_s[...] = eightfold(hot[0] + hot[1])
        count_s[...] = eightfold(count)
        gate_s[...] = eightfold(hot[0] * gates[0:1, :] + hot[1] * gates[1:2, :])
        cot_s[...] = stacked(cot)

    here = slot_here(count_s[...], piece)
    rows = jnp.where(here, gate_s[...], 0.0)
    send[...] = jnp.dot(spread(rows), cot_s[...], preferred_element_type=F32).astype(BF)
    turned[...] = spread_turned(jnp.where(here, hot_s[...], 0.0).T)


def combine_kernel(turned, back, out):
    total = sum(
        jnp.dot(
            turned[p * PACKED : (p + 1) * PACKED, :],
            back[:, p * WIDE : (p + 1) * WIDE],
            preferred_element_type=F32,
        )
        for p in range(PIECES)
    ).astype(BF)
    for c in range(SHARDS):
        out[:, c * WIDE : (c + 1) * WIDE] = total[c * TOK : (c + 1) * TOK, :]


def packing(member, turned):
    shape = (256, 256)
    outer, inner = iota(shape, 1 if turned else 0), iota(shape, 0 if turned else 1)
    within = outer % 64
    chunk = (member + outer // 64) % SHARDS
    return (inner == (within // 2) * 8 + chunk * 2 + within % 2).astype(BF)


def unpack(packed, order, blocks, piece):
    for half in range(2):
        block = jnp.dot(
            order,
            packed[half * 256 : half * 256 + 256, piece * WIDE : (piece + 1) * WIDE],
            preferred_element_type=F32,
        ).astype(BF)
        start = (piece * 2 + half) * 64
        for k in range(SHARDS):
            blocks[k][start : start + 64, :] = block[k * 64 : k * 64 + 64, :]


def copies_of(parts, dest, sems, base):
    own, right, opp_a, opp_b, left = parts
    half = opp_a.shape[0]
    pairs = (
        (own, dest.at[0]),
        (right, dest.at[1]),
        (opp_a, dest.at[2, pl.ds(0, half)]),
        (opp_b, dest.at[2, pl.ds(half, half)]),
        (left, dest.at[3]),
    )
    return [pltpu.make_async_copy(s, d, sems.at[base + n]) for n, (s, d) in enumerate(pairs)]


def begin(copies):
    for copy in copies:
        copy.start()


def finish(copies):
    for copy in copies:
        copy.wait()


def unpack_kernel(info, recv, *blocks):
    order = packing(info[0], False)
    for piece in range(PIECES):
        unpack(recv, order, blocks, piece)


def forward_kernel(info, *refs):
    blocks = refs[0:4]
    gate_parts, up_parts = refs[4:9], refs[9:14]
    hidden, slope_gate, slope_up = refs[14:17]
    gate_v, up_v, sems = refs[17:]
    copies = copies_of(gate_parts, gate_v, sems, 0) + copies_of(up_parts, up_v, sems, 5)
    begin(copies)
    finish(copies)
    pre_gate = jnp.zeros((ROWS, HID), F32)
    pre_up = jnp.zeros((ROWS, HID), F32)
    for k in range(SHARDS):
        x = blocks[k][...]
        pre_gate += jnp.dot(x, gate_v[k], preferred_element_type=F32)
        pre_up += jnp.dot(x, up_v[k], preferred_element_type=F32)
    sigma = jax.nn.sigmoid(pre_gate)
    silu = pre_gate * sigma
    live = iota((ROWS, HID), 1) < info[1]
    hidden[...] = jnp.where(live, silu * pre_up, 0.0).astype(BF)
    slope_gate[...] = jnp.where(live, pre_up * sigma * (1.0 + pre_gate * (1.0 - sigma)), 0.0)
    slope_up[...] = jnp.where(live, silu, 0.0)


def dot_turned(x, w):
    return lax.dot_general(x, w, (((1,), (1,)), ((), ())), preferred_element_type=F32)


def backward_kernel(info, recv, slope_gate, slope_up, *refs):
    down_parts, gate_parts, up_parts = refs[0:5], refs[5:10], refs[10:15]
    rows_out = refs[15:19]
    d_gate, d_up, send = refs[19:22]
    recv_v, slope_gate_v, slope_up_v, down_v, gate_v, up_v = refs[22:28]
    blocks = refs[28:32]
    held, send_v, sems = refs[32:]
    columns = [pl.ds(piece * WIDE, WIDE) for piece in range(PIECES)]
    loads = [
        pltpu.make_async_copy(recv.at[:, columns[n]], recv_v.at[:, columns[n]], sems.at[25 + n])
        for n in range(PIECES)
    ]
    down = copies_of(down_parts, down_v, sems, 3)
    slopes = [
        pltpu.make_async_copy(slope_gate, slope_gate_v, sems.at[1]),
        pltpu.make_async_copy(slope_up, slope_up_v, sems.at[2]),
    ]
    gate = copies_of(gate_parts, gate_v, sems, 8)
    up = copies_of(up_parts, up_v, sems, 13)
    begin(loads)
    order = packing(info[0], False)
    loads[0].wait()
    begin(down[:2])
    unpack(recv_v, order, blocks, 0)
    loads[1].wait()
    begin(down[2:])
    unpack(recv_v, order, blocks, 1)
    loads[2].wait()
    begin(slopes)
    unpack(recv_v, order, blocks, 2)
    shards = ((0,), (1,), (2, 3), (4,))
    grad = jnp.zeros((ROWS, HID), F32)
    for k in range(SHARDS):
        for n in shards[k]:
            down[n].wait()
            gate[n].start()
            up[n].start()
        grad += dot_turned(blocks[k][...], down_v[k])
    finish(slopes)
    outs = [
        pltpu.make_async_copy(blocks[k], rows_out[k], sems.at[18 + k]) for k in range(SHARDS)
    ]
    d_gate[...] = (grad * slope_gate_v[...]).astype(BF)
    d_up[...] = (grad * slope_up_v[...]).astype(BF)
    for k in range(SHARDS):
        for n in shards[k]:
            gate[n].wait()
            up[n].wait()
        outs[k].start()
        part = (
            dot_turned(d_gate[...], gate_v[k]) + dot_turned(d_up[...], up_v[k])
        ).astype(BF)
        for n in range(2 * PIECES):
            held[n * 256 + k * 64 : n * 256 + k * 64 + 64, :] = part[n * 64 : n * 64 + 64, :]
    back = packing(info[0], True)
    for piece in range(PIECES):
        for half in range(2):
            start = (piece * 2 + half) * 256
            send_v[piece, half * 256 : half * 256 + 256, :] = jnp.dot(
                back, held[start : start + 256, :], preferred_element_type=F32
            ).astype(BF)
        copy = pltpu.make_async_copy(
            send_v.at[piece], send.at[:, columns[piece]], sems.at[22 + piece]
        )
        copy.start()
        outs.append(copy)
    finish(outs)


RIGHT = [(n, (n + 1) % SHARDS) for n in range(SHARDS)]
LEFT = [(n, (n - 1) % SHARDS) for n in range(SHARDS)]


def to_right(x):
    return lax.ppermute(x, "dp", RIGHT)


def to_left(x):
    return lax.ppermute(x, "dp", LEFT)


def near(own):
    return to_right(own), to_left(own)


def far(left, right):
    half = left.shape[0] // 2
    return to_right(left[:half]), to_left(right[half:])


def scatter(own, right, opp, left, beside):
    half = opp.shape[0] // 2
    narrow = lambda v: v.astype(BF)
    wide = lambda v: v.astype(F32)
    from_left = to_right(narrow(opp[:half]))
    from_right = to_left(narrow(opp[half:]))
    left_b = to_right(narrow(right[half:]))
    right_a = to_left(narrow(left[:half]))
    left_a = to_right(narrow(right[:half] + wide(from_left)))
    right_b = to_left(narrow(left[half:] + wide(from_right)))
    done, left_a, right_b = lax.optimization_barrier((beside(), left_a, right_b))
    top = narrow(own[:half] + wide(left_a) + wide(right_a))
    bottom = narrow(own[half:] + wide(left_b) + wide(right_b))
    return jnp.concatenate([top, bottom], axis=0), done


def exchange(x):
    return lax.all_to_all(
        x.reshape(CORES, 8, PIECES * WIDE), "expert", split_axis=0, concat_axis=0, tiled=True
    ).reshape(PACKED, PIECES * WIDE)


PACKED_TYPE = jax.ShapeDtypeStruct((PACKED, PIECES * WIDE), BF)
BLOCK_TYPE = jax.ShapeDtypeStruct((ROWS, WIDE), BF)
HID_BF = jax.ShapeDtypeStruct((ROWS, HID), BF)
HID_F32 = jax.ShapeDtypeStruct((ROWS, HID), F32)
WEIGHT = pltpu.VMEM((SHARDS, WIDE, HID), BF)
PACKED_V = pltpu.VMEM((PACKED, PIECES * WIDE), BF)
MAPPED = pltpu.VMEM((PACKED, TOK), F32)
TALL = pltpu.VMEM((PACKED, WIDE), BF)
TURNED_ROWS = pl.BlockSpec((PACKED, PACKED), lambda p: (p, 0))
PIECE_COLS = pl.BlockSpec((PACKED, WIDE), lambda p: (0, p))


def whole(*shape):
    return pl.BlockSpec(shape, lambda p: (0, 0))


def call(kernel, flops, nbytes, mib, name, **rest):
    return pl.pallas_call(
        kernel,
        compiler_params=pltpu.CompilerParams(vmem_limit_bytes=mib * MIB),
        cost_estimate=pl.CostEstimate(flops=flops, bytes_accessed=nbytes, transcendentals=0),
        name=name,
        **rest,
    )


def run_route(ids, place, tokens):
    return call(
        route_kernel, 1_700_000_000, 5_000_000, 62, "route",
        grid=(PIECES,),
        in_specs=[whole(2, TOK), whole(1, CORES), whole(TOK, SHARDS * WIDE)],
        out_specs=PIECE_COLS,
        out_shape=PACKED_TYPE,
        scratch_shapes=[MAPPED, MAPPED, TALL],
    )(ids, place, tokens)


def run_scale(ids, place, gates, cotangent):
    return call(
        scale_kernel, 1_700_000_000, 6_000_000, 62, "scale",
        grid=(PIECES,),
        in_specs=[whole(2, TOK), whole(1, CORES), whole(2, TOK), whole(TOK, SHARDS * WIDE)],
        out_specs=[PIECE_COLS, TURNED_ROWS],
        out_shape=[PACKED_TYPE, jax.ShapeDtypeStruct((PIECES * PACKED, PACKED), BF)],
        scratch_shapes=[MAPPED, MAPPED, MAPPED, TALL],
    )(ids, place, gates, cotangent)


def run_unpack(info, recv):
    return call(
        unpack_kernel, 800_000_000, 6_000_000, 62, "unpack",
        in_specs=[SMEM, VMEM],
        out_specs=[VMEM] * 4,
        out_shape=[BLOCK_TYPE] * 4,
    )(info, recv)


def run_forward(info, blocks, gate_parts, up_parts):
    return call(
        forward_kernel, 3_300_000_000, 14_000_000, 62, "forward",
        in_specs=[SMEM] + [VMEM] * 4 + [ANY] * 10,
        out_specs=[VMEM] * 3,
        out_shape=[HID_BF, HID_F32, HID_F32],
        scratch_shapes=[WEIGHT, WEIGHT, pltpu.SemaphoreType.DMA((10,))],
    )(info, *blocks, *gate_parts, *up_parts)


def run_backward(info, recv, slope_gate, slope_up, down_parts, gate_parts, up_parts):
    return call(
        backward_kernel, 7_000_000_000, 26_000_000, 62, "backward",
        in_specs=[SMEM] + [ANY] * 18,
        out_specs=[ANY] * 4 + [VMEM, VMEM, ANY],
        out_shape=[BLOCK_TYPE] * 4 + [HID_BF, HID_BF, PACKED_TYPE],
        scratch_shapes=[
            PACKED_V,
            pltpu.VMEM((ROWS, HID), F32),
            pltpu.VMEM((ROWS, HID), F32),
            pltpu.VMEM((SHARDS, HID, WIDE), BF),
            WEIGHT,
            WEIGHT,
            *[pltpu.VMEM((ROWS, WIDE), BF)] * 4,
            pltpu.VMEM((2 * PIECES * 256, WIDE), BF),
            pltpu.VMEM((PIECES, PACKED, WIDE), BF),
            pltpu.SemaphoreType.DMA((28,)),
        ],
    )(info, recv, slope_gate, slope_up, *down_parts, *gate_parts, *up_parts)


def run_combine(turned, recv):
    return call(
        combine_kernel, 1_700_000_000, 5_000_000, 16, "combine",
        in_specs=[VMEM] * 2,
        out_specs=VMEM,
        out_shape=jax.ShapeDtypeStruct((TOK, SHARDS * WIDE), BF),
    )(turned, recv)


def on_device(tokens, cotangent, expert_ids, gates, widths, placement, w_gate, w_up, w_down):
    experts = jnp.arange(CORES, dtype=jnp.int32)
    owner = jnp.sum(jnp.where(placement == lax.axis_index("expert"), experts, 0))
    width = jnp.sum(jnp.where(experts == owner, widths, 0))
    info = jnp.stack([lax.axis_index("dp").astype(jnp.int32), width])
    shards = (w_gate[0], w_up[0], w_down[0])
    nears = [near(w) for w in shards]
    ids = expert_ids.T
    place = placement[None]

    recv_x = exchange(run_route(ids, place, tokens))
    send_g, turned = run_scale(ids, place, gates.astype(F32).T, cotangent)
    send_g, nears, info = lax.optimization_barrier((send_g, nears, info))
    recv_g = exchange(send_g)
    parts = []
    for own, (left, right) in zip(shards, nears):
        opp_a, opp_b = far(left, right)
        parts.append((own, right, opp_a, opp_b, left))
    gate_parts, up_parts, down_parts = parts

    blocks_x = run_unpack(info, recv_x)
    mid = ROWS // 2
    x_left, x_right = to_right(blocks_x[1]), to_left(blocks_x[3])
    x_passing = to_right(blocks_x[2][:mid]), to_left(blocks_x[2][mid:])

    hidden, slope_gate, slope_up = run_forward(info, blocks_x, gate_parts, up_parts)
    recv_g, x_left, x_right, x_passing = lax.optimization_barrier(
        (recv_g, x_left, x_right, x_passing)
    )
    x_far = to_right(x_passing[0]), to_left(x_passing[1])

    *blocks_g, d_gate, d_up, send_d = run_backward(
        info, recv_g, slope_gate, slope_up, down_parts, gate_parts, up_parts
    )
    recv_d = exchange(send_d)

    dot = functools.partial(jnp.einsum, "ra,rb->ab", preferred_element_type=F32)

    def summed(d):
        left, right = near(d)
        opp_a, opp_b = far(left, right)
        return (
            dot(blocks_x[0], d)
            + dot(x_left, left)
            + dot(x_right, right)
            + dot(x_far[0], opp_a)
            + dot(x_far[1], opp_b)
        ).astype(BF)

    grad_gate = summed(d_gate)
    grad_up = summed(d_up)
    grad_down, grad_tokens = scatter(
        *[dot(hidden, block) for block in blocks_g], lambda: run_combine(turned, recv_d)
    )
    return (grad_tokens, grad_gate[None], grad_up[None], grad_down[None])


def solution(mesh):
    placed = (
        P(("dp", "expert"), None),
        P(("dp", "expert"), None),
        P(("dp", "expert"), None),
        P(("dp", "expert"), None),
        P(),
        P(),
        P("expert", "dp", None),
        P("expert", "dp", None),
        P("expert", None, "dp"),
    )
    return jax.shard_map(
        on_device,
        mesh=mesh,
        in_specs=placed,
        out_specs=(
            P(("dp", "expert"), None),
            P("expert", "dp", None),
            P("expert", "dp", None),
            P("expert", None, "dp"),
        ),
        check_vma=False,
    )
```

```python
import functools

import jax
import jax.numpy as jnp
from jax import lax
from jax.experimental import pallas as pl
from jax.experimental.pallas import tpu as pltpu
from jax.sharding import PartitionSpec as P

BF = jnp.bfloat16
F32 = jnp.float32
SHARDS = 4
SLOTS = 6
PIECES = 3
CORES = 64
TOK = 128
WIDE = 1024
HID = 512
ROWS = CORES * SLOTS
PACKED = CORES * 8
VMEM = pl.BlockSpec(memory_space=pltpu.VMEM)
SMEM = pl.BlockSpec(memory_space=pltpu.SMEM)
ANY = pl.BlockSpec(memory_space=pl.ANY)
MIB = 1024 * 1024


def iota(shape, dim):
    return lax.broadcasted_iota(jnp.int32, shape, dim)


def spread(rows):
    chunk = (iota((PACKED, TOK), 0) % 8) // 2
    return jnp.concatenate(
        [jnp.where(chunk == c, rows, 0.0).astype(BF) for c in range(SHARDS)], axis=1
    )


def spread_turned(rows):
    chunk = (iota((TOK, PACKED), 1) % 8) // 2
    return jnp.concatenate(
        [jnp.where(chunk == c, rows, 0.0).astype(BF) for c in range(SHARDS)], axis=0
    )


def stacked(ref):
    return jnp.concatenate([ref[:, c * WIDE : (c + 1) * WIDE] for c in range(SHARDS)], axis=0)


def routing(ids, place):
    expert = iota((CORES, TOK), 0)
    slot_of = (iota((CORES, CORES), 0) == place[0:1, :]).astype(BF)
    hot = [
        jnp.dot(slot_of, (ids[k : k + 1, :] == expert).astype(BF), preferred_element_type=F32)
        for k in range(2)
    ]
    before = (iota((TOK, TOK), 0) < iota((TOK, TOK), 1)).astype(BF)
    count = jnp.dot((hot[0] + hot[1]).astype(BF), before, preferred_element_type=F32)
    return hot, count


def eightfold(x):
    return jnp.broadcast_to(x[:, None, :], (CORES, 8, TOK)).reshape(PACKED, TOK)


def slot_here(count, piece):
    return count == (2 * piece + iota((PACKED, TOK), 0) % 2).astype(F32)


def route_kernel(ids, place, tok, send, hot_s, count_s, tok_s):
    piece = pl.program_id(0)

    @pl.when(piece == 0)
    def _():
        hot, count = routing(ids, place)
        hot_s[...] = eightfold(hot[0] + hot[1])
        count_s[...] = eightfold(count)
        tok_s[...] = stacked(tok)

    rows = jnp.where(slot_here(count_s[...], piece), hot_s[...], 0.0)
    send[...] = jnp.dot(spread(rows), tok_s[...], preferred_element_type=F32).astype(BF)


def scale_kernel(ids, place, gates, cot, send, turned, hot_s, count_s, gate_s, cot_s):
    piece = pl.program_id(0)

    @pl.when(piece == 0)
    def _():
        hot, count = routing(ids, place)
        hot_s[...] = eightfold(hot[0] + hot[1])
        count_s[...] = eightfold(count)
        gate_s[...] = eightfold(hot[0] * gates[0:1, :] + hot[1] * gates[1:2, :])
        cot_s[...] = stacked(cot)

    here = slot_here(count_s[...], piece)
    rows = jnp.where(here, gate_s[...], 0.0)
    send[...] = jnp.dot(spread(rows), cot_s[...], preferred_element_type=F32).astype(BF)
    turned[...] = spread_turned(jnp.where(here, hot_s[...], 0.0).T)


def combine_kernel(turned, back, out):
    total = sum(
        jnp.dot(
            turned[p * PACKED : (p + 1) * PACKED, :],
            back[:, p * WIDE : (p + 1) * WIDE],
            preferred_element_type=F32,
        )
        for p in range(PIECES)
    ).astype(BF)
    for c in range(SHARDS):
        out[:, c * WIDE : (c + 1) * WIDE] = total[c * TOK : (c + 1) * TOK, :]


def packing(member, turned):
    shape = (256, 256)
    outer, inner = iota(shape, 1 if turned else 0), iota(shape, 0 if turned else 1)
    within = outer % 64
    chunk = (member + outer // 64) % SHARDS
    return (inner == (within // 2) * 8 + chunk * 2 + within % 2).astype(BF)


def unpack(packed, order, blocks, piece):
    for half in range(2):
        block = jnp.dot(
            order,
            packed[half * 256 : half * 256 + 256, piece * WIDE : (piece + 1) * WIDE],
            preferred_element_type=F32,
        ).astype(BF)
        start = (piece * 2 + half) * 64
        for k in range(SHARDS):
            blocks[k][start : start + 64, :] = block[k * 64 : k * 64 + 64, :]


def copies_of(parts, dest, sems, base):
    own, right, opp_a, opp_b, left = parts
    half = opp_a.shape[0]
    pairs = (
        (own, dest.at[0]),
        (right, dest.at[1]),
        (opp_a, dest.at[2, pl.ds(0, half)]),
        (opp_b, dest.at[2, pl.ds(half, half)]),
        (left, dest.at[3]),
    )
    return [pltpu.make_async_copy(s, d, sems.at[base + n]) for n, (s, d) in enumerate(pairs)]


def begin(copies):
    for copy in copies:
        copy.start()


def finish(copies):
    for copy in copies:
        copy.wait()


def unpack_kernel(info, recv, *blocks):
    order = packing(info[0], False)
    for piece in range(PIECES):
        unpack(recv, order, blocks, piece)


def forward_kernel(info, *refs):
    blocks = refs[0:4]
    gate_parts, up_parts = refs[4:9], refs[9:14]
    hidden, slope_gate, slope_up = refs[14:17]
    gate_v, up_v, sems = refs[17:]
    copies = copies_of(gate_parts, gate_v, sems, 0) + copies_of(up_parts, up_v, sems, 5)
    begin(copies)
    finish(copies)
    pre_gate = jnp.zeros((ROWS, HID), F32)
    pre_up = jnp.zeros((ROWS, HID), F32)
    for k in range(SHARDS):
        x = blocks[k][...]
        pre_gate += jnp.dot(x, gate_v[k], preferred_element_type=F32)
        pre_up += jnp.dot(x, up_v[k], preferred_element_type=F32)
    sigma = jax.nn.sigmoid(pre_gate)
    silu = pre_gate * sigma
    live = iota((ROWS, HID), 1) < info[1]
    hidden[...] = jnp.where(live, silu * pre_up, 0.0).astype(BF)
    slope_gate[...] = jnp.where(live, pre_up * sigma * (1.0 + pre_gate * (1.0 - sigma)), 0.0)
    slope_up[...] = jnp.where(live, silu, 0.0)


def dot_turned(x, w):
    return lax.dot_general(x, w, (((1,), (1,)), ((), ())), preferred_element_type=F32)


def backward_kernel(info, recv, slope_gate, slope_up, *refs):
    down_parts, gate_parts, up_parts = refs[0:5], refs[5:10], refs[10:15]
    rows_out = refs[15:19]
    d_gate, d_up, send = refs[19:22]
    recv_v, slope_gate_v, slope_up_v, down_v, gate_v, up_v = refs[22:28]
    blocks = refs[28:32]
    held, send_v, sems = refs[32:]
    columns = [pl.ds(piece * WIDE, WIDE) for piece in range(PIECES)]
    loads = [
        pltpu.make_async_copy(recv.at[:, columns[n]], recv_v.at[:, columns[n]], sems.at[25 + n])
        for n in range(PIECES)
    ]
    down = copies_of(down_parts, down_v, sems, 3)
    slopes = [
        pltpu.make_async_copy(slope_gate, slope_gate_v, sems.at[1]),
        pltpu.make_async_copy(slope_up, slope_up_v, sems.at[2]),
    ]
    gate = copies_of(gate_parts, gate_v, sems, 8)
    up = copies_of(up_parts, up_v, sems, 13)
    begin(loads)
    order = packing(info[0], False)
    loads[0].wait()
    begin(down[:2])
    unpack(recv_v, order, blocks, 0)
    loads[1].wait()
    begin(down[2:])
    unpack(recv_v, order, blocks, 1)
    loads[2].wait()
    begin(slopes)
    for n in range(5):
        gate[n].start()
        up[n].start()
    unpack(recv_v, order, blocks, 2)
    shards = ((0,), (1,), (2, 3), (4,))
    grad = jnp.zeros((ROWS, HID), F32)
    for k in range(SHARDS):
        for n in shards[k]:
            down[n].wait()
        grad += dot_turned(blocks[k][...], down_v[k])
    finish(slopes)
    outs = [
        pltpu.make_async_copy(blocks[k], rows_out[k], sems.at[18 + k]) for k in range(SHARDS)
    ]
    d_gate[...] = (grad * slope_gate_v[...]).astype(BF)
    d_up[...] = (grad * slope_up_v[...]).astype(BF)
    for k in range(SHARDS):
        for n in shards[k]:
            gate[n].wait()
            up[n].wait()
        outs[k].start()
        part = (
            dot_turned(d_gate[...], gate_v[k]) + dot_turned(d_up[...], up_v[k])
        ).astype(BF)
        for n in range(2 * PIECES):
            held[n * 256 + k * 64 : n * 256 + k * 64 + 64, :] = part[n * 64 : n * 64 + 64, :]
    back = packing(info[0], True)
    for piece in range(PIECES):
        for half in range(2):
            start = (piece * 2 + half) * 256
            send_v[piece, half * 256 : half * 256 + 256, :] = jnp.dot(
                back, held[start : start + 256, :], preferred_element_type=F32
            ).astype(BF)
        copy = pltpu.make_async_copy(
            send_v.at[piece], send.at[:, columns[piece]], sems.at[22 + piece]
        )
        copy.start()
        outs.append(copy)
    finish(outs)


RIGHT = [(n, (n + 1) % SHARDS) for n in range(SHARDS)]
LEFT = [(n, (n - 1) % SHARDS) for n in range(SHARDS)]


def to_right(x):
    return lax.ppermute(x, "dp", RIGHT)


def to_left(x):
    return lax.ppermute(x, "dp", LEFT)


def near(own):
    return to_right(own), to_left(own)


def far(left, right):
    half = left.shape[0] // 2
    return to_right(left[:half]), to_left(right[half:])


def scatter(own, right, opp, left, beside):
    half = opp.shape[0] // 2
    narrow = lambda v: v.astype(BF)
    wide = lambda v: v.astype(F32)
    from_left = to_right(narrow(opp[:half]))
    from_right = to_left(narrow(opp[half:]))
    left_b = to_right(narrow(right[half:]))
    right_a = to_left(narrow(left[:half]))
    left_a = to_right(narrow(right[:half] + wide(from_left)))
    right_b = to_left(narrow(left[half:] + wide(from_right)))
    done, left_a, right_b = lax.optimization_barrier((beside(), left_a, right_b))
    top = narrow(own[:half] + wide(left_a) + wide(right_a))
    bottom = narrow(own[half:] + wide(left_b) + wide(right_b))
    return jnp.concatenate([top, bottom], axis=0), done


def exchange(x):
    return lax.all_to_all(
        x.reshape(CORES, 8, PIECES * WIDE), "expert", split_axis=0, concat_axis=0, tiled=True
    ).reshape(PACKED, PIECES * WIDE)


PACKED_TYPE = jax.ShapeDtypeStruct((PACKED, PIECES * WIDE), BF)
BLOCK_TYPE = jax.ShapeDtypeStruct((ROWS, WIDE), BF)
HID_BF = jax.ShapeDtypeStruct((ROWS, HID), BF)
HID_F32 = jax.ShapeDtypeStruct((ROWS, HID), F32)
WEIGHT = pltpu.VMEM((SHARDS, WIDE, HID), BF)
PACKED_V = pltpu.VMEM((PACKED, PIECES * WIDE), BF)
MAPPED = pltpu.VMEM((PACKED, TOK), F32)
TALL = pltpu.VMEM((PACKED, WIDE), BF)
TURNED_ROWS = pl.BlockSpec((PACKED, PACKED), lambda p: (p, 0))
PIECE_COLS = pl.BlockSpec((PACKED, WIDE), lambda p: (0, p))


def whole(*shape):
    return pl.BlockSpec(shape, lambda p: (0, 0))


def call(kernel, flops, nbytes, mib, name, **rest):
    return pl.pallas_call(
        kernel,
        compiler_params=pltpu.CompilerParams(vmem_limit_bytes=mib * MIB),
        cost_estimate=pl.CostEstimate(flops=flops, bytes_accessed=nbytes, transcendentals=0),
        name=name,
        **rest,
    )


def run_route(ids, place, tokens):
    return call(
        route_kernel, 1_700_000_000, 5_000_000, 62, "route",
        grid=(PIECES,),
        in_specs=[whole(2, TOK), whole(1, CORES), whole(TOK, SHARDS * WIDE)],
        out_specs=PIECE_COLS,
        out_shape=PACKED_TYPE,
        scratch_shapes=[MAPPED, MAPPED, TALL],
    )(ids, place, tokens)


def run_scale(ids, place, gates, cotangent):
    return call(
        scale_kernel, 1_700_000_000, 6_000_000, 62, "scale",
        grid=(PIECES,),
        in_specs=[whole(2, TOK), whole(1, CORES), whole(2, TOK), whole(TOK, SHARDS * WIDE)],
        out_specs=[PIECE_COLS, TURNED_ROWS],
        out_shape=[PACKED_TYPE, jax.ShapeDtypeStruct((PIECES * PACKED, PACKED), BF)],
        scratch_shapes=[MAPPED, MAPPED, MAPPED, TALL],
    )(ids, place, gates, cotangent)


def run_unpack(info, recv):
    return call(
        unpack_kernel, 800_000_000, 6_000_000, 62, "unpack",
        in_specs=[SMEM, VMEM],
        out_specs=[VMEM] * 4,
        out_shape=[BLOCK_TYPE] * 4,
    )(info, recv)


def run_forward(info, blocks, gate_parts, up_parts):
    return call(
        forward_kernel, 3_300_000_000, 14_000_000, 62, "forward",
        in_specs=[SMEM] + [VMEM] * 4 + [ANY] * 10,
        out_specs=[VMEM] * 3,
        out_shape=[HID_BF, HID_F32, HID_F32],
        scratch_shapes=[WEIGHT, WEIGHT, pltpu.SemaphoreType.DMA((10,))],
    )(info, *blocks, *gate_parts, *up_parts)


def run_backward(info, recv, slope_gate, slope_up, down_parts, gate_parts, up_parts):
    return call(
        backward_kernel, 7_000_000_000, 26_000_000, 62, "backward",
        in_specs=[SMEM] + [ANY] * 18,
        out_specs=[ANY] * 4 + [VMEM, VMEM, ANY],
        out_shape=[BLOCK_TYPE] * 4 + [HID_BF, HID_BF, PACKED_TYPE],
        scratch_shapes=[
            PACKED_V,
            pltpu.VMEM((ROWS, HID), F32),
            pltpu.VMEM((ROWS, HID), F32),
            pltpu.VMEM((SHARDS, HID, WIDE), BF),
            WEIGHT,
            WEIGHT,
            *[pltpu.VMEM((ROWS, WIDE), BF)] * 4,
            pltpu.VMEM((2 * PIECES * 256, WIDE), BF),
            pltpu.VMEM((PIECES, PACKED, WIDE), BF),
            pltpu.SemaphoreType.DMA((28,)),
        ],
    )(info, recv, slope_gate, slope_up, *down_parts, *gate_parts, *up_parts)


def run_combine(turned, recv):
    return call(
        combine_kernel, 1_700_000_000, 5_000_000, 16, "combine",
        in_specs=[VMEM] * 2,
        out_specs=VMEM,
        out_shape=jax.ShapeDtypeStruct((TOK, SHARDS * WIDE), BF),
    )(turned, recv)


def on_device(tokens, cotangent, expert_ids, gates, widths, placement, w_gate, w_up, w_down):
    experts = jnp.arange(CORES, dtype=jnp.int32)
    owner = jnp.sum(jnp.where(placement == lax.axis_index("expert"), experts, 0))
    width = jnp.sum(jnp.where(experts == owner, widths, 0))
    info = jnp.stack([lax.axis_index("dp").astype(jnp.int32), width])
    shards = (w_gate[0], w_up[0], w_down[0])
    nears = [near(w) for w in shards]
    ids = expert_ids.T
    place = placement[None]

    recv_x = exchange(run_route(ids, place, tokens))
    send_g, turned = run_scale(ids, place, gates.astype(F32).T, cotangent)
    send_g, nears, info = lax.optimization_barrier((send_g, nears, info))
    recv_g = exchange(send_g)
    parts = []
    for own, (left, right) in zip(shards, nears):
        opp_a, opp_b = far(left, right)
        parts.append((own, right, opp_a, opp_b, left))
    gate_parts, up_parts, down_parts = parts

    blocks_x = run_unpack(info, recv_x)
    mid = ROWS // 2
    x_left, x_right = to_right(blocks_x[1]), to_left(blocks_x[3])
    x_passing = to_right(blocks_x[2][:mid]), to_left(blocks_x[2][mid:])

    hidden, slope_gate, slope_up = run_forward(info, blocks_x, gate_parts, up_parts)
    recv_g, x_left, x_right, x_passing = lax.optimization_barrier(
        (recv_g, x_left, x_right, x_passing)
    )
    x_far = to_right(x_passing[0]), to_left(x_passing[1])

    *blocks_g, d_gate, d_up, send_d = run_backward(
        info, recv_g, slope_gate, slope_up, down_parts, gate_parts, up_parts
    )
    recv_d = exchange(send_d)

    dot = functools.partial(jnp.einsum, "ra,rb->ab", preferred_element_type=F32)

    def summed(d):
        left, right = near(d)
        opp_a, opp_b = far(left, right)
        return (
            dot(blocks_x[0], d)
            + dot(x_left, left)
            + dot(x_right, right)
            + dot(x_far[0], opp_a)
            + dot(x_far[1], opp_b)
        ).astype(BF)

    grad_gate = summed(d_gate)
    grad_up = summed(d_up)
    grad_down, grad_tokens = scatter(
        *[dot(hidden, block) for block in blocks_g], lambda: run_combine(turned, recv_d)
    )
    return (grad_tokens, grad_gate[None], grad_up[None], grad_down[None])


def solution(mesh):
    placed = (
        P(("dp", "expert"), None),
        P(("dp", "expert"), None),
        P(("dp", "expert"), None),
        P(("dp", "expert"), None),
        P(),
        P(),
        P("expert", "dp", None),
        P("expert", "dp", None),
        P("expert", None, "dp"),
    )
    return jax.shard_map(
        on_device,
        mesh=mesh,
        in_specs=placed,
        out_specs=(
            P(("dp", "expert"), None),
            P("expert", "dp", None),
            P("expert", "dp", None),
            P("expert", None, "dp"),
        ),
        check_vma=False,
    )
```
